512 devices in a mesh: section: 2 (over x_hi), blk: 128 (over y, x_lo, z), sta: 2 (over core).
Axes of the slice: x: 4 (x_hi: 2, x_lo: 2; x = x_hi * 2 + x_lo), y: 4, z: 16, core: 2. Of those that a mesh axis runs over, the one named last changes fastest.
Arguments:
- raw_traces: bfloat16 [1200, 327680], P(('section', 'sta'), 'blk'), may hold values from -600 to 600
- fir_taps: bfloat16 [60], replicated, may hold values from -0.75 to 0.75
- templates: bfloat16 [128, 1200, 256], P('blk', ('section', 'sta')), may hold values from -600 to 600
- start_offsets: int32 [128], P('blk'), may hold values from 0 to 128, as said below
- channel_mask: int32 [128, 1200], P('blk', ('section', 'sta')), may hold values from 0 to 1, as said below
- station_shifts: int32 [400], P(('section', 'sta')), may hold values from 0 to 64, as said below
Outputs:
- detection: float32 [128, 65536], P(('section', 'sta'), 'blk')
The draws below stay inside these ranges and needn't reach their ends.
Inputs may be any that keep to these rules, and one draw needn't show every extreme that they name: `start_offsets`: some template starts at the last possible sample. `channel_mask`: every template uses at least one channel. `station_shifts`: some station has the shift 64.
All inputs are finite; a program needn't handle non-finite values.
Results may differ from the reference program's by a relative error of at most 0.0029.
Values may be sent and summed in bfloat16 or wider, within the bound.
No kernel may reach another device: no remote copies, remote signals or barrier semaphores. Data moves between devices by JAX's collectives and lax.ppermute only.
A program may use at most 128 MiB of HBM per device.

```python
import math
import jax
import jax.numpy as jnp
from jax import lax

STATIONS = 400
CHANNEL_COUNT = 1200
TLEN = 128
TWIN = 256
NTAP = 60
DECIM = 5
SHIFT_MAX = 64
TPL = 128
DAY = 65536
RAW_SAMPLES = 327680


def draw_raw_traces(key, part):
    key = jax.random.fold_in(key, 11)
    background_key, amplitude_key, transient_key = jax.random.split(key, 3)
    array_shape = (CHANNEL_COUNT, RAW_SAMPLES)
    noise_floor = jnp.clip(jax.random.normal(background_key, array_shape, jnp.float32), -6.0, 6.0)
    slope_rate = 2.0
    channel_scales = jnp.exp(jax.random.uniform(amplitude_key, (CHANNEL_COUNT, 1), jnp.float32, 0.0, math.log(10.0)))
    position = jnp.arange(RAW_SAMPLES, dtype=jnp.float32) / RAW_SAMPLES
    drift_slope = jnp.sqrt(1.0 + slope_rate * position)[None, :]
    trace_pieces = (RAW_SAMPLES + 63) // 64
    transients = jnp.exp(jax.random.uniform(transient_key, (CHANNEL_COUNT, trace_pieces), jnp.float32, 0.0, math.log(3.0)))
    transient_rows = jnp.repeat(transients, 64, axis=1)[:, :RAW_SAMPLES]
    return (noise_floor * channel_scales * drift_slope * transient_rows).astype(jnp.bfloat16)


def draw_templates(key, part):
    key = jax.random.fold_in(key, 23)
    background_key, chan_key, time_key = jax.random.split(key, 3)
    array_shape = (TPL, CHANNEL_COUNT, TWIN)
    noise_floor = jnp.clip(jax.random.normal(background_key, array_shape, jnp.float32), -6.0, 6.0)
    chan_scale = jnp.exp(jax.random.uniform(chan_key, (TPL, CHANNEL_COUNT, 1), jnp.float32, 0.0, math.log(10.0)))
    time_scale = jnp.exp(jax.random.uniform(time_key, (TPL, 1, TWIN), jnp.float32, 0.0, math.log(10.0)))
    return (noise_floor * chan_scale * time_scale).astype(jnp.bfloat16)


def draw_start_offsets(key, part):
    key = jax.random.fold_in(key, 37)
    value_key, pick_key = jax.random.split(key, 2)
    drawn = jax.random.randint(value_key, (TPL,), 0, TWIN - TLEN + 1)
    chosen = jax.random.randint(pick_key, (), 0, TPL)
    return jnp.where(jnp.arange(TPL) == chosen, TWIN - TLEN, drawn).astype(jnp.int32)


def draw_channel_mask(key, part):
    key = jax.random.fold_in(key, 41)
    rate_key, value_key, pick_key = jax.random.split(key, 3)
    rates = jax.random.randint(rate_key, (TPL, 1), 50, 101)
    values = jax.random.randint(value_key, (TPL, CHANNEL_COUNT), 0, 100)
    picked = jax.random.randint(pick_key, (TPL, 1), 0, CHANNEL_COUNT)
    kept = (values < rates) | (jnp.arange(CHANNEL_COUNT)[None, :] == picked)
    return kept.astype(jnp.int32)


def draw_station_shifts(key, part):
    key = jax.random.fold_in(key, 53)
    value_key, pick_key = jax.random.split(key, 2)
    drawn = jax.random.randint(value_key, (STATIONS,), 0, SHIFT_MAX + 1)
    chosen = jax.random.randint(pick_key, (), 0, STATIONS)
    return jnp.where(jnp.arange(STATIONS) == chosen, SHIFT_MAX, drawn).astype(jnp.int32)


def noise(own_key, dims, width, bound, held_as=jnp.bfloat16):
    entries = jax.random.normal(own_key, dims, jnp.float32) * width
    return jnp.minimum(jnp.maximum(entries, -bound), bound).astype(held_as)


def setup_inputs(seed: int = 0) -> dict:
    splits = jax.random.split(jax.random.key(seed), 7)
    raw_traces = draw_raw_traces(jax.random.fold_in(splits[6], 71), 0)
    fir_taps = noise(splits[1], (NTAP,), NTAP ** -0.5, 0.75)
    templates = draw_templates(jax.random.fold_in(splits[6], 71), 0)
    start_offsets = draw_start_offsets(jax.random.fold_in(splits[6], 71), 0)
    channel_mask = draw_channel_mask(jax.random.fold_in(splits[6], 71), 0)
    station_shifts = draw_station_shifts(jax.random.fold_in(splits[6], 71), 0)
    return {"raw_traces": raw_traces, "fir_taps": fir_taps, "templates": templates, "start_offsets": start_offsets, "channel_mask": channel_mask, "station_shifts": station_shifts}


def skew_sum(product, lag_count):
    groups, taps_len, span_len = product.shape
    flat_vals = product.reshape(groups, taps_len * span_len)
    cut_at = (taps_len - 1) * (span_len + 1)
    lead_rows = flat_vals[:, :cut_at].reshape(groups, taps_len - 1, span_len + 1)[:, :, :lag_count]
    last_row = flat_vals[:, cut_at:cut_at + lag_count]
    return lax.optimization_barrier(jnp.sum(lead_rows, axis=1)) + last_row

def cut_one(stored, begin_at, keep_flags):
    window = lax.dynamic_slice_in_dim(stored, begin_at.astype(jnp.int32), TLEN, axis=1)
    return window * keep_flags.astype(jnp.bfloat16)[:, None]

def shift_row(trace_row, lag_shift):
    return lax.dynamic_slice_in_dim(trace_row, lag_shift.astype(jnp.int32), DAY + TLEN - 1)

def reference(raw_traces, fir_taps, templates, start_offsets, channel_mask, station_shifts):
    raw_float = raw_traces.astype(jnp.float32)
    tap_float = fir_taps.astype(jnp.float32)
    phases = NTAP // DECIM
    padded = jnp.pad(raw_float, ((0, 0), (0, DECIM * phases)))
    polyphase = padded.reshape(CHANNEL_COUNT, DAY + phases, DECIM)
    decimated = jnp.zeros((CHANNEL_COUNT, DAY), jnp.float32)
    for phase_idx in range(phases):
        decimated = decimated + jnp.dot(polyphase[:, phase_idx:phase_idx + DAY, :], tap_float[phase_idx * DECIM:(phase_idx + 1) * DECIM], precision=lax.Precision.HIGHEST)
    powers = lax.optimization_barrier(jnp.sum(decimated * decimated, axis=1))
    root_power = jnp.sqrt(powers / DAY + 1e-06)
    trace_rows = (decimated / root_power[:, None]).astype(jnp.bfloat16)
    rim_len = TLEN - 1 + SHIFT_MAX
    extended = jnp.pad(trace_rows, ((0, 0), (0, rim_len)))
    chan_shift = jnp.repeat(station_shifts, 3)
    shifted = jax.vmap(shift_row)(extended, chan_shift).astype(jnp.float32)
    panels = jax.vmap(cut_one)(templates, start_offsets, channel_mask)

    def per_template(panel):
        panel_float = panel.astype(jnp.float32)
        product = jnp.dot(panel_float.T, shifted, precision=lax.Precision.HIGHEST)
        corr_row = skew_sum(product[None], DAY)[0]
        norm_sum = jnp.sum(panel_float * panel_float)
        return corr_row / jnp.sqrt(norm_sum + 1e-05)
    return lax.map(per_template, panels)
```

```python
import functools

import jax
import jax.numpy as jnp
import numpy as np
from jax import lax
from jax.experimental import pallas as pl
from jax.experimental.pallas import tpu as pltpu
from jax.sharding import Mesh, PartitionSpec as P

TLEN = 128
NTAP = 60
DECIM = 5
SHIFT_MAX = 64
LANES = 128
SUB = 16
ROWS = TLEN // SUB
PAIR = 2
WIDE = 640
GROUPS = 8
GROUP = 40
BLK = ("y", "xl", "zq", "zp")


def vmem():
    return pl.BlockSpec(memory_space=pltpu.VMEM)


def params(mib):
    return pltpu.CompilerParams(vmem_limit_bytes=mib << 20)


def from_next_block(value):
    count = 128
    return lax.ppermute(value, BLK, [(i + 1, i) for i in range(count - 1)])


def tap_matrix(fir_taps):
    depth = DECIM * LANES + LANES
    pattern = jnp.concatenate([fir_taps, jnp.zeros((depth + DECIM - NTAP,), fir_taps.dtype)])
    flat = jnp.tile(pattern, LANES)[: LANES * depth]
    return flat.reshape(LANES, depth)


def decimate_kernel(raw_ref, rim_ref, weights_ref, out_ref):
    step = DECIM * LANES
    blocks = out_ref.shape[1] // LANES
    dims = (((1,), (1,)), ((), ()))
    for i in range(blocks):
        if i < blocks - 1:
            part = lax.dot_general(
                raw_ref[:, i * step : i * step + step + LANES], weights_ref[...], dims,
                preferred_element_type=jnp.float32,
            )
        else:
            part = lax.dot_general(
                raw_ref[:, i * step :], weights_ref[:, :step], dims,
                preferred_element_type=jnp.float32,
            ) + lax.dot_general(
                rim_ref[...], weights_ref[:, step:], dims,
                preferred_element_type=jnp.float32,
            )
        out_ref[:, i * LANES : (i + 1) * LANES] = part


def shift_kernel(dec_ref, rim_ref, root_ref, shift_ref, out_ref):
    channels = dec_ref.shape[0]
    rows = jnp.concatenate([dec_ref[...], rim_ref[...]], axis=1)
    rows = (rows / root_ref[...]).astype(jnp.bfloat16).astype(jnp.float32)
    shift = shift_ref[...]
    width = rows.shape[1]
    for bit in range(SHIFT_MAX.bit_length()):
        step = 1 << bit
        moved = pltpu.roll(rows, width - step, 1)
        rows = jnp.where((shift & step) != 0, moved, rows)
    rows = rows[:, :WIDE]
    tail = jnp.zeros((out_ref.shape[0] - channels, WIDE), jnp.float32)
    out_ref[...] = jnp.concatenate([rows, tail], axis=0).astype(jnp.bfloat16)


def corr_kernel(panel_ref, first_ref, second_ref, trace_ref, out_ref, mixed, panels, shifted):
    chunks = panel_ref.shape[0] // LANES
    lags = out_ref.shape[-1]
    depth = PAIR * SUB * GROUP
    count = ROWS // PAIR

    @pl.when(pl.program_id(0) == 0)
    def _():
        for i in range(chunks):
            part = jnp.dot(
                first_ref[...], panel_ref[i * LANES : (i + 1) * LANES, :],
                preferred_element_type=jnp.float32,
            ).astype(jnp.bfloat16)
            for r in range(ROWS):
                mixed[r, i * SUB : (i + 1) * SUB, :] = part[r * SUB : (r + 1) * SUB, :]
        for r in range(ROWS):
            part = jnp.dot(
                second_ref[...], mixed[r], preferred_element_type=jnp.float32
            ).astype(jnp.bfloat16)
            a, h = divmod(r, PAIR)
            panels[a * LANES : (a + 1) * LANES, h * WIDE : (h + 1) * WIDE] = part

    pieces = trace_ref.shape[0]
    for t in range(pieces):
        trace = trace_ref[t].astype(jnp.float32)
        for j in range(PAIR * SUB // 2):
            low = trace if j == 0 else pltpu.roll(trace, WIDE - 2 * j, 1)
            high = pltpu.roll(trace, WIDE - 2 * j - 1, 1)
            both = jnp.concatenate([low, high], axis=0).astype(jnp.bfloat16)
            shifted[j * 2 * GROUP : (j + 1) * 2 * GROUP, t * WIDE : (t + 1) * WIDE] = both
    sums = jnp.dot(panels[...], shifted[...], preferred_element_type=jnp.float32)
    for t in range(pieces):
        total = sums[:LANES, t * WIDE : t * WIDE + lags]
        for a in range(1, count):
            part = sums[a * LANES : (a + 1) * LANES, t * WIDE : (t + 1) * WIDE]
            total = total + pltpu.roll(part, WIDE - a * PAIR * SUB, 1)[:, :lags]
        for c in range(2):
            for x in range(2):
                g = c * 2 + x
                out_ref[c, x, t] = total[g * 32 : (g + 1) * 32, :]


def orders():
    first = np.zeros((LANES, LANES), np.float32)
    for src in range(SUB):
        for r in range(ROWS):
            first[r * SUB + src, src * ROWS + r] = 1
    second = np.zeros((LANES, LANES), np.float32)
    for zq in range(8):
        for y in range(4):
            for xl in range(2):
                for zp in range(2):
                    source = ((zq * 4 + y) * 2 + xl) * 2 + zp
                    x, c = divmod(y, 2)
                    target = (((c * 2 + x) * 2 + xl) * 8 + zq) * 2 + zp
                    second[target, source] = 1
    return jnp.asarray(first, jnp.bfloat16), jnp.asarray(second, jnp.bfloat16)


def correlate(gathered, traces, lags):
    first, second = orders()
    pieces = 2
    depth = PAIR * SUB * GROUP
    whole = lambda shape: pl.BlockSpec(shape, lambda i: (0,) * len(shape))
    flops = 2 * ROWS // PAIR * LANES * depth * WIDE * GROUPS
    return pl.pallas_call(
        corr_kernel,
        grid=(GROUPS // pieces,),
        in_specs=[
            whole(gathered.shape),
            whole(first.shape),
            whole(second.shape),
            pl.BlockSpec((pieces, GROUP, WIDE), lambda i: (i, 0, 0)),
        ],
        out_specs=pl.BlockSpec((2, 2, pieces, 32, lags), lambda i: (0, 0, i, 0, 0)),
        out_shape=jax.ShapeDtypeStruct((2, 2, GROUPS, 32, lags), jnp.float32),
        scratch_shapes=[
            pltpu.VMEM((ROWS, LANES, WIDE), jnp.bfloat16),
            pltpu.VMEM((ROWS // PAIR * LANES, depth), jnp.bfloat16),
            pltpu.VMEM((depth, pieces * WIDE), jnp.bfloat16),
        ],
        compiler_params=params(48),
        cost_estimate=pl.CostEstimate(flops=flops, bytes_accessed=4 << 20, transcendentals=0),
    )(gathered, first, second, traces)


def local(raw_traces, fir_taps, templates, start_offsets, channel_mask, station_shifts):
    channels, raw_len = raw_traces.shape
    lags = raw_len // DECIM
    blocks = lax.axis_size(BLK)
    raw_rim = from_next_block(raw_traces[:, :LANES])

    window = lax.dynamic_slice_in_dim(templates[0], start_offsets[0], TLEN, axis=1)
    panel = window * channel_mask[0].astype(jnp.bfloat16)[:, None]
    own_norm = jnp.sum(jnp.square(panel.astype(jnp.float32)))
    padded = jnp.pad(panel, ((0, GROUPS * GROUP - channels), (0, 0)))
    message = padded.reshape(GROUPS, GROUP, ROWS, SUB).transpose(0, 2, 3, 1)
    message = message.reshape(GROUPS, 1, ROWS, SUB * GROUP)
    message = jnp.broadcast_to(message, (GROUPS, 2, ROWS, SUB * GROUP))
    message = message.reshape(2 * GROUPS, ROWS, SUB * GROUP)
    exchanged = lax.all_to_all(message, ("y", "xl", "zp"), 0, 0, tiled=True)
    gathered = lax.all_gather(exchanged, "zq", axis=0, tiled=True)
    gathered = gathered.reshape(blocks * ROWS, SUB * GROUP)

    decimated = pl.pallas_call(
        decimate_kernel,
        in_specs=[vmem()] * 3,
        out_specs=vmem(),
        out_shape=jax.ShapeDtypeStruct((channels, lags), jnp.float32),
        compiler_params=params(32),
    )(raw_traces, raw_rim, tap_matrix(fir_taps))
    rim = from_next_block(decimated[:, : 2 * LANES])
    own_power = jnp.sum(decimated * decimated, axis=1)
    own_facts = jnp.concatenate([own_power, own_norm[None], jnp.zeros((3,), jnp.float32)])
    facts = lax.all_to_all(
        jnp.broadcast_to(own_facts[None], (blocks, own_facts.shape[0])), BLK, 0, 0, tiled=True
    )
    powers = jnp.sum(facts[:, :channels], axis=0)
    root_power = jnp.sqrt(powers / (lags * blocks) + 1e-06)
    part_norms = facts[:, channels].reshape(4, 32)
    norms = jnp.sum(lax.all_to_all(part_norms, ("xh", "core"), 0, 0, tiled=True), axis=0)

    traces = pl.pallas_call(
        shift_kernel,
        in_specs=[vmem()] * 4,
        out_specs=vmem(),
        out_shape=jax.ShapeDtypeStruct((GROUPS * GROUP, WIDE), jnp.bfloat16),
        compiler_params=params(32),
    )(decimated, rim, root_power[:, None], jnp.repeat(station_shifts, 3)[:, None])
    traces = lax.all_to_all(
        traces.reshape(GROUPS, GROUP, WIDE), ("y", "xl"), 0, 0, tiled=True
    )

    sums = correlate(gathered, traces, lags)
    sums = jnp.sum(lax.all_to_all(sums, "core", 0, 0, tiled=True), axis=0)
    sums = sums.reshape(2 * GROUPS, 32, lags)
    sums = jnp.sum(lax.all_to_all(sums, ("xh", "y", "xl"), 0, 0, tiled=True), axis=0)
    return sums / jnp.sqrt(norms + 1e-05)[:, None]


def solution(mesh):
    fine = Mesh(
        mesh.devices.reshape(2, 4, 2, 8, 2, 2), ("xh", "y", "xl", "zq", "zp", "core")
    )
    parts = ("xh", "core")
    return jax.shard_map(
        local,
        mesh=fine,
        in_specs=(P(parts, BLK), P(), P(BLK, parts, None), P(BLK), P(BLK, parts), P(parts)),
        out_specs=P(parts, BLK),
        check_vma=False,
    )
```

```python
import jax
import jax.numpy as jnp
import numpy as np
from jax import lax
from jax.experimental import pallas as pl
from jax.experimental.pallas import tpu as pltpu
from jax.sharding import Mesh, PartitionSpec as P

TLEN = 128
NTAP = 60
DECIM = 5
SHIFT_MAX = 64
LANES = 128
SUB = 16
ROWS = TLEN // SUB
PAIR = 2
WIDE = 640
GROUPS = 8
GROUP = 40
USED = 38
RIM = 1024
PIECES = 2
BLK = ("y", "xl", "zq", "zp")


def vmem():
    return pl.BlockSpec(memory_space=pltpu.VMEM)


def params(mib):
    return pltpu.CompilerParams(vmem_limit_bytes=mib << 20)


def from_next_block(value):
    count = 128
    return lax.ppermute(value, BLK, [(i + 1, i) for i in range(count - 1)])


def tap_matrix(fir_taps):
    depth = DECIM * LANES + LANES
    pattern = jnp.concatenate([fir_taps, jnp.zeros((depth + DECIM - NTAP,), fir_taps.dtype)])
    flat = jnp.tile(pattern, LANES)[: LANES * depth]
    return flat.reshape(LANES, depth)


def trace_kernel(norm_ref, raw_ref, rim_ref, weights_ref, shift_ref, out_ref):
    channels = raw_ref.shape[0]
    step = DECIM * LANES
    own = raw_ref.shape[1] // step
    dims = (((1,), (1,)), ((), ()))

    def product(left, right):
        return lax.dot_general(left, right, dims, preferred_element_type=jnp.float32)

    blocks = []
    for i in range(own - 1):
        blocks.append(product(raw_ref[:, i * step : i * step + step + LANES], weights_ref[...]))
    blocks.append(
        product(raw_ref[:, (own - 1) * step :], weights_ref[:, :step])
        + product(rim_ref[:, :LANES], weights_ref[:, step:])
    )
    blocks.append(product(rim_ref[:, : step + LANES], weights_ref[...]))
    blocks.append(product(rim_ref[:, step:], weights_ref[:, : RIM - step]))
    squares = blocks[0] * blocks[0]
    for block in blocks[1:own]:
        squares = squares + block * block
    power = jnp.sum(squares, axis=1, keepdims=True)

    rows = jnp.concatenate(blocks, axis=1)
    shift = shift_ref[...]
    width = rows.shape[1]
    for bit in range(SHIFT_MAX.bit_length()):
        hop = 1 << bit
        moved = pltpu.roll(rows, width - hop, 1)
        rows = jnp.where((shift & hop) != 0, moved, rows)
    rows = rows[:, :WIDE]
    lane = lax.broadcasted_iota(jnp.int32, rows.shape, 1)
    rows = jnp.where(lane == WIDE - 1, power, rows)
    spare = GROUP - USED
    side = lax.broadcasted_iota(jnp.int32, (spare, WIDE), 0)
    side = jnp.where(side == 0, norm_ref[0], 0.0)
    for g in range(GROUPS):
        first, last = g * USED, min((g + 1) * USED, channels)
        pieces = [rows[first:last]]
        if last - first < USED:
            pieces.append(jnp.zeros((USED - last + first, WIDE), jnp.float32))
        out_ref[g] = jnp.concatenate(pieces + [side], axis=0)


def spread_kernel(trace_ref, root_ref, out_ref):
    pieces = trace_ref.shape[0]
    for t in range(pieces):
        trace = (trace_ref[t] / root_ref[...]).astype(jnp.bfloat16).astype(jnp.float32)
        for j in range(PAIR * SUB // 2):
            low = trace if j == 0 else pltpu.roll(trace, WIDE - 2 * j, 1)
            high = pltpu.roll(trace, WIDE - 2 * j - 1, 1)
            both = jnp.concatenate([low, high], axis=0).astype(jnp.bfloat16)
            out_ref[0, j * 2 * GROUP : (j + 1) * 2 * GROUP, t * WIDE : (t + 1) * WIDE] = both


def corr_kernel(panel_ref, first_ref, second_ref, shifted_ref, out_ref, mixed, panels):
    chunks = panel_ref.shape[0] // LANES
    lags = out_ref.shape[-1]
    count = ROWS // PAIR

    @pl.when(pl.program_id(0) == 0)
    def _():
        for i in range(chunks):
            part = jnp.dot(
                first_ref[...], panel_ref[i * LANES : (i + 1) * LANES, :],
                preferred_element_type=jnp.float32,
            ).astype(jnp.bfloat16)
            for r in range(ROWS):
                mixed[r, i * SUB : (i + 1) * SUB, :] = part[r * SUB : (r + 1) * SUB, :]
        for r in range(ROWS):
            part = jnp.dot(
                second_ref[...], mixed[r], preferred_element_type=jnp.float32
            ).astype(jnp.bfloat16)
            a, h = divmod(r, PAIR)
            panels[a * LANES : (a + 1) * LANES, h * WIDE : (h + 1) * WIDE] = part

    pieces = out_ref.shape[2]
    sums = jnp.dot(panels[...], shifted_ref[0], preferred_element_type=jnp.float32)
    for t in range(pieces):
        total = sums[:LANES, t * WIDE : t * WIDE + lags]
        for a in range(1, count):
            part = sums[a * LANES : (a + 1) * LANES, t * WIDE : (t + 1) * WIDE]
            total = total + pltpu.roll(part, WIDE - a * PAIR * SUB, 1)[:, :lags]
        for c in range(2):
            for x in range(2):
                g = c * 2 + x
                out_ref[c, x, t] = total[g * 32 : (g + 1) * 32, :]


def orders():
    first = np.zeros((LANES, LANES), np.float32)
    for src in range(SUB):
        for r in range(ROWS):
            first[r * SUB + src, src * ROWS + r] = 1
    second = np.zeros((LANES, LANES), np.float32)
    for zq in range(8):
        for y in range(4):
            for xl in range(2):
                for zp in range(2):
                    source = ((zq * 4 + y) * 2 + xl) * 2 + zp
                    x, c = divmod(y, 2)
                    target = (((c * 2 + x) * 2 + xl) * 8 + zq) * 2 + zp
                    second[target, source] = 1
    return jnp.asarray(first, jnp.bfloat16), jnp.asarray(second, jnp.bfloat16)


def whole(shape):
    return pl.BlockSpec(shape, lambda i: (0,) * len(shape))


def spread(traces, root_power):
    depth = PAIR * SUB * GROUP
    return pl.pallas_call(
        spread_kernel,
        grid=(GROUPS // PIECES,),
        in_specs=[
            pl.BlockSpec((PIECES, GROUP, WIDE), lambda i: (i, 0, 0)),
            whole(root_power.shape),
        ],
        out_specs=pl.BlockSpec((1, depth, PIECES * WIDE), lambda i: (i, 0, 0)),
        out_shape=jax.ShapeDtypeStruct((GROUPS // PIECES, depth, PIECES * WIDE), jnp.bfloat16),
        compiler_params=params(32),
        cost_estimate=pl.CostEstimate(flops=20 << 20, bytes_accessed=14 << 20, transcendentals=0),
    )(traces, root_power)


def correlate(gathered, shifted, lags):
    first, second = orders()
    depth = PAIR * SUB * GROUP
    flops = 2 * ROWS // PAIR * LANES * depth * WIDE * GROUPS
    return pl.pallas_call(
        corr_kernel,
        grid=(GROUPS // PIECES,),
        in_specs=[
            whole(gathered.shape),
            whole(first.shape),
            whole(second.shape),
            pl.BlockSpec((1,) + shifted.shape[1:], lambda i: (i, 0, 0)),
        ],
        out_specs=pl.BlockSpec((2, 2, PIECES, 32, lags), lambda i: (0, 0, i, 0, 0)),
        out_shape=jax.ShapeDtypeStruct((2, 2, GROUPS, 32, lags), jnp.float32),
        scratch_shapes=[
            pltpu.VMEM((ROWS, LANES, WIDE), jnp.bfloat16),
            pltpu.VMEM((ROWS // PAIR * LANES, depth), jnp.bfloat16),
        ],
        compiler_params=params(48),
        cost_estimate=pl.CostEstimate(flops=flops, bytes_accessed=17 << 20, transcendentals=0),
    )(gathered, first, second, shifted)


def local(raw_traces, fir_taps, templates, start_offsets, channel_mask, station_shifts):
    channels, raw_len = raw_traces.shape
    lags = raw_len // DECIM
    blocks = lax.axis_size(BLK)
    raw_rim = from_next_block(raw_traces[:, :RIM])

    window = lax.dynamic_slice_in_dim(templates[0], start_offsets[0], TLEN, axis=1)
    panel = window * channel_mask[0].astype(jnp.bfloat16)[:, None]
    norm = jnp.sum(jnp.square(panel.astype(jnp.float32)))[None]
    padded = jnp.pad(panel, ((0, GROUPS * USED - channels), (0, 0)))
    padded = jnp.pad(padded.reshape(GROUPS, USED, TLEN), ((0, 0), (0, GROUP - USED), (0, 0)))
    message = padded.reshape(GROUPS, GROUP, ROWS, SUB).transpose(0, 2, 3, 1)
    message = message.reshape(GROUPS, 1, ROWS, SUB * GROUP)
    message = jnp.broadcast_to(message, (GROUPS, 2, ROWS, SUB * GROUP))
    message = message.reshape(2 * GROUPS, ROWS, SUB * GROUP)
    exchanged = lax.all_to_all(message, ("y", "xl", "zp"), 0, 0, tiled=True)
    gathered = lax.all_gather(exchanged, "zq", axis=0, tiled=True)
    gathered = gathered.reshape(blocks * ROWS, SUB * GROUP)

    norm = norm + lax.ppermute(norm, "core", [(0, 1), (1, 0)])
    norm = norm + lax.ppermute(norm, "xh", [(0, 1), (1, 0)])

    traces = pl.pallas_call(
        trace_kernel,
        in_specs=[pl.BlockSpec(memory_space=pltpu.SMEM)] + [vmem()] * 4,
        out_specs=vmem(),
        out_shape=jax.ShapeDtypeStruct((GROUPS, GROUP, WIDE), jnp.float32),
        compiler_params=params(32),
        cost_estimate=pl.CostEstimate(flops=400 << 20, bytes_accessed=4 << 20, transcendentals=0),
    )(norm, raw_traces, raw_rim, tap_matrix(fir_taps), jnp.repeat(station_shifts, 3)[:, None])
    traces = lax.all_to_all(traces, ("y", "xl"), 0, 0, tiled=True)

    powers = jnp.sum(traces[:, :, WIDE - 1], axis=0)
    norms = traces[:, USED, 0]
    facts = jnp.concatenate([powers, norms, jnp.zeros((LANES - GROUP - GROUPS,), jnp.float32)])
    along = lax.axis_size(("zq", "zp"))
    facts = jnp.broadcast_to(facts[None], (along, LANES))
    facts = lax.all_to_all(facts, ("zq", "zp"), 0, 0, tiled=True)
    powers = jnp.sum(facts[:, :GROUP], axis=0)
    root_power = jnp.sqrt(powers / (lags * blocks) + 1e-06)
    norms = facts[:, GROUP : GROUP + GROUPS].T.reshape(4, 2 * along)
    norms = lax.dynamic_index_in_dim(norms, lax.axis_index(("xh", "core")), 0, keepdims=False)

    shifted = spread(traces, root_power[:, None])
    sums = correlate(gathered, shifted, lags)
    sums = jnp.sum(lax.all_to_all(sums, "core", 0, 0, tiled=True), axis=0)
    sums = sums.reshape(2 * GROUPS, 32, lags)
    sums = jnp.sum(lax.all_to_all(sums, ("xh", "y", "xl"), 0, 0, tiled=True), axis=0)
    return sums / jnp.sqrt(norms + 1e-05)[:, None]


def solution(mesh):
    fine = Mesh(
        mesh.devices.reshape(2, 4, 2, 8, 2, 2), ("xh", "y", "xl", "zq", "zp", "core")
    )
    parts = ("xh", "core")
    return jax.shard_map(
        local,
        mesh=fine,
        in_specs=(P(parts, BLK), P(), P(BLK, parts, None), P(BLK), P(BLK, parts), P(parts)),
        out_specs=P(parts, BLK),
        check_vma=False,
    )
```

```python
import jax
import jax.numpy as jnp
import numpy as np
from jax import lax
from jax.experimental import pallas as pl
from jax.experimental.pallas import tpu as pltpu
from jax.sharding import Mesh, PartitionSpec as P

TLEN = 128
NTAP = 60
DECIM = 5
SHIFT_MAX = 64
LANES = 128
SUB = 16
ROWS = TLEN // SUB
PAIR = 2
WIDE = 640
GROUPS = 8
GROUP = 40
USED = 38
RIM = 1024
PIECES = 2
BLK = ("y", "xl", "zq", "zp")


def vmem():
    return pl.BlockSpec(memory_space=pltpu.VMEM)


def params(mib):
    return pltpu.CompilerParams(vmem_limit_bytes=mib << 20)


def from_next_block(value):
    count = 128
    return lax.ppermute(value, BLK, [(i + 1, i) for i in range(count - 1)])


def tap_matrix(fir_taps):
    depth = DECIM * LANES + LANES
    pattern = jnp.concatenate([fir_taps, jnp.zeros((depth + DECIM - NTAP,), fir_taps.dtype)])
    flat = jnp.tile(pattern, LANES)[: LANES * depth]
    return flat.reshape(LANES, depth)


def trace_kernel(norm_ref, raw_ref, rim_ref, weights_ref, shift_ref, out_ref):
    channels = raw_ref.shape[0]
    step = DECIM * LANES
    own = raw_ref.shape[1] // step
    dims = (((1,), (1,)), ((), ()))

    def product(left, right):
        return lax.dot_general(left, right, dims, preferred_element_type=jnp.float32)

    blocks = []
    for i in range(own - 1):
        blocks.append(product(raw_ref[:, i * step : i * step + step + LANES], weights_ref[...]))
    blocks.append(
        product(raw_ref[:, (own - 1) * step :], weights_ref[:, :step])
        + product(rim_ref[:, :LANES], weights_ref[:, step:])
    )
    blocks.append(product(rim_ref[:, : step + LANES], weights_ref[...]))
    blocks.append(product(rim_ref[:, step:], weights_ref[:, : RIM - step]))
    squares = blocks[0] * blocks[0]
    for block in blocks[1:own]:
        squares = squares + block * block
    power = jnp.sum(squares, axis=1, keepdims=True)

    rows = jnp.concatenate(blocks, axis=1)
    shift = shift_ref[...]
    width = rows.shape[1]
    for bit in range(SHIFT_MAX.bit_length()):
        hop = 1 << bit
        moved = pltpu.roll(rows, width - hop, 1)
        rows = jnp.where((shift & hop) != 0, moved, rows)
    rows = rows[:, :WIDE]
    lane = lax.broadcasted_iota(jnp.int32, rows.shape, 1)
    rows = jnp.where(lane == WIDE - 1, power, rows)
    spare = GROUP - USED
    side = lax.broadcasted_iota(jnp.int32, (spare, WIDE), 0)
    side = jnp.where(side == 0, norm_ref[0], 0.0)
    for g in range(GROUPS):
        first, last = g * USED, min((g + 1) * USED, channels)
        pieces = [rows[first:last]]
        if last - first < USED:
            pieces.append(jnp.zeros((USED - last + first, WIDE), jnp.float32))
        out_ref[g] = jnp.concatenate(pieces + [side], axis=0)


def corr_kernel(
    panel_ref, first_ref, second_ref, trace_ref, root_ref, out_ref, mixed, panels, shifted
):
    chunks = panel_ref.shape[0] // LANES
    lags = out_ref.shape[-1]
    count = ROWS // PAIR

    @pl.when(pl.program_id(0) == 0)
    def _():
        for i in range(chunks):
            part = jnp.dot(
                first_ref[...], panel_ref[i * LANES : (i + 1) * LANES, :],
                preferred_element_type=jnp.float32,
            ).astype(jnp.bfloat16)
            for r in range(ROWS):
                mixed[r, i * SUB : (i + 1) * SUB, :] = part[r * SUB : (r + 1) * SUB, :]
        for r in range(ROWS):
            part = jnp.dot(
                second_ref[...], mixed[r], preferred_element_type=jnp.float32
            ).astype(jnp.bfloat16)
            a, h = divmod(r, PAIR)
            panels[a * LANES : (a + 1) * LANES, h * WIDE : (h + 1) * WIDE] = part

    pieces = trace_ref.shape[0]
    for t in range(pieces):
        trace = (trace_ref[t] / root_ref[...]).astype(jnp.bfloat16).astype(jnp.float32)
        for j in range(PAIR * SUB // 2):
            low = trace if j == 0 else pltpu.roll(trace, WIDE - 2 * j, 1)
            high = pltpu.roll(trace, WIDE - 2 * j - 1, 1)
            both = jnp.concatenate([low, high], axis=0).astype(jnp.bfloat16)
            shifted[j * 2 * GROUP : (j + 1) * 2 * GROUP, t * WIDE : (t + 1) * WIDE] = both
    sums = jnp.dot(panels[...], shifted[...], preferred_element_type=jnp.float32)
    for t in range(pieces):
        total = sums[:LANES, t * WIDE : t * WIDE + lags]
        for a in range(1, count):
            part = sums[a * LANES : (a + 1) * LANES, t * WIDE : (t + 1) * WIDE]
            total = total + pltpu.roll(part, WIDE - a * PAIR * SUB, 1)[:, :lags]
        for c in range(2):
            for x in range(2):
                g = c * 2 + x
                out_ref[c, x, t] = total[g * 32 : (g + 1) * 32, :]


def orders():
    first = np.zeros((LANES, LANES), np.float32)
    for src in range(SUB):
        for r in range(ROWS):
            first[r * SUB + src, src * ROWS + r] = 1
    second = np.zeros((LANES, LANES), np.float32)
    for zq in range(8):
        for y in range(4):
            for xl in range(2):
                for zp in range(2):
                    source = ((zq * 4 + y) * 2 + xl) * 2 + zp
                    x, c = divmod(y, 2)
                    target = (((c * 2 + x) * 2 + xl) * 8 + zq) * 2 + zp
                    second[target, source] = 1
    return jnp.asarray(first, jnp.bfloat16), jnp.asarray(second, jnp.bfloat16)


def whole(shape):
    return pl.BlockSpec(shape, lambda i: (0,) * len(shape))


def correlate(gathered, traces, root_power, lags):
    first, second = orders()
    depth = PAIR * SUB * GROUP
    flops = 2 * ROWS // PAIR * LANES * depth * WIDE * GROUPS
    return pl.pallas_call(
        corr_kernel,
        grid=(GROUPS // PIECES,),
        in_specs=[
            whole(gathered.shape),
            whole(first.shape),
            whole(second.shape),
            pl.BlockSpec((PIECES, GROUP, WIDE), lambda i: (i, 0, 0)),
            whole(root_power.shape),
        ],
        out_specs=pl.BlockSpec((2, 2, PIECES, 32, lags), lambda i: (0, 0, i, 0, 0)),
        out_shape=jax.ShapeDtypeStruct((2, 2, GROUPS, 32, lags), jnp.float32),
        scratch_shapes=[
            pltpu.VMEM((ROWS, LANES, WIDE), jnp.bfloat16),
            pltpu.VMEM((ROWS // PAIR * LANES, depth), jnp.bfloat16),
            pltpu.VMEM((depth, PIECES * WIDE), jnp.bfloat16),
        ],
        compiler_params=params(48),
        cost_estimate=pl.CostEstimate(flops=flops, bytes_accessed=4 << 20, transcendentals=0),
    )(gathered, first, second, traces, root_power)


def local(raw_traces, fir_taps, templates, start_offsets, channel_mask, station_shifts):
    channels, raw_len = raw_traces.shape
    lags = raw_len // DECIM
    blocks = lax.axis_size(BLK)
    raw_rim = from_next_block(raw_traces[:, :RIM])

    window = lax.dynamic_slice_in_dim(templates[0], start_offsets[0], TLEN, axis=1)
    panel = window * channel_mask[0].astype(jnp.bfloat16)[:, None]
    norm = jnp.sum(jnp.square(panel.astype(jnp.float32)))[None]
    padded = jnp.pad(panel, ((0, GROUPS * USED - channels), (0, 0)))
    padded = jnp.pad(padded.reshape(GROUPS, USED, TLEN), ((0, 0), (0, GROUP - USED), (0, 0)))
    message = padded.reshape(GROUPS, GROUP, ROWS, SUB).transpose(0, 2, 3, 1)
    message = message.reshape(GROUPS, 1, ROWS, SUB * GROUP)
    message = jnp.broadcast_to(message, (GROUPS, 2, ROWS, SUB * GROUP))
    message = message.reshape(2 * GROUPS, ROWS, SUB * GROUP)
    exchanged = lax.all_to_all(message, ("y", "xl", "zp"), 0, 0, tiled=True)
    exchanged, raw_rim = lax.optimization_barrier((exchanged, raw_rim))
    gathered = lax.all_gather(exchanged, "zq", axis=0, tiled=True)
    gathered = gathered.reshape(blocks * ROWS, SUB * GROUP)

    norm = norm + lax.ppermute(norm, "core", [(0, 1), (1, 0)])
    norm = norm + lax.ppermute(norm, "xh", [(0, 1), (1, 0)])

    traces = pl.pallas_call(
        trace_kernel,
        in_specs=[pl.BlockSpec(memory_space=pltpu.SMEM)] + [vmem()] * 4,
        out_specs=vmem(),
        out_shape=jax.ShapeDtypeStruct((GROUPS, GROUP, WIDE), jnp.float32),
        compiler_params=params(32),
        cost_estimate=pl.CostEstimate(flops=400 << 20, bytes_accessed=4 << 20, transcendentals=0),
    )(norm, raw_traces, raw_rim, tap_matrix(fir_taps), jnp.repeat(station_shifts, 3)[:, None])
    traces = lax.all_to_all(traces, ("y", "xl"), 0, 0, tiled=True)

    powers = jnp.sum(traces[:, :, WIDE - 1], axis=0)
    norms = traces[:, USED, 0]
    facts = jnp.concatenate([powers, norms, jnp.zeros((LANES - GROUP - GROUPS,), jnp.float32)])
    along = lax.axis_size(("zq", "zp"))
    facts = jnp.broadcast_to(facts[None], (along, LANES))
    facts = lax.all_to_all(facts, ("zq", "zp"), 0, 0, tiled=True)
    powers = jnp.sum(facts[:, :GROUP], axis=0)
    root_power = jnp.sqrt(powers / (lags * blocks) + 1e-06)
    norms = facts[:, GROUP : GROUP + GROUPS].T.reshape(4, 2 * along)
    norms = lax.dynamic_index_in_dim(norms, lax.axis_index(("xh", "core")), 0, keepdims=False)

    sums = correlate(gathered, traces, root_power[:, None], lags)
    sums = jnp.sum(lax.all_to_all(sums, "core", 0, 0, tiled=True), axis=0)
    sums = sums.astype(jnp.bfloat16).reshape(2 * GROUPS, 32, lags)
    sums = lax.all_to_all(sums, ("xh", "y", "xl"), 0, 0, tiled=True)
    sums = jnp.sum(sums.astype(jnp.float32), axis=0)
    return sums / jnp.sqrt(norms + 1e-05)[:, None]


def solution(mesh):
    fine = Mesh(
        mesh.devices.reshape(2, 4, 2, 8, 2, 2), ("xh", "y", "xl", "zq", "zp", "core")
    )
    parts = ("xh", "core")
    return jax.shard_map(
        local,
        mesh=fine,
        in_specs=(P(parts, BLK), P(), P(BLK, parts, None), P(BLK), P(BLK, parts), P(parts)),
        out_specs=P(parts, BLK),
        check_vma=False,
    )
```

```python
import jax
import jax.numpy as jnp
import numpy as np
from jax import lax
from jax.experimental import pallas as pl
from jax.experimental.pallas import tpu as pltpu
from jax.sharding import Mesh, PartitionSpec as P

TLEN = 128
NTAP = 60
DECIM = 5
SHIFT_MAX = 64
LANES = 128
SUB = 16
ROWS = TLEN // SUB
PAIR = 2
WIDE = 640
GROUPS = 8
GROUP = 40
USED = 38
RIM = 192
PIECES = 2
BLK = ("y", "xl", "zq", "zp")


def vmem():
    return pl.BlockSpec(memory_space=pltpu.VMEM)


def params(mib):
    return pltpu.CompilerParams(vmem_limit_bytes=mib << 20)


def from_next_block(value):
    count = 128
    return lax.ppermute(value, BLK, [(i + 1, i) for i in range(count - 1)])


def tap_matrix(fir_taps):
    depth = DECIM * LANES + LANES
    pattern = jnp.concatenate([fir_taps, jnp.zeros((depth + DECIM - NTAP,), fir_taps.dtype)])
    flat = jnp.tile(pattern, LANES)[: LANES * depth]
    return flat.reshape(LANES, depth)


def product(left, right):
    dims = (((1,), (1,)), ((), ()))
    return lax.dot_general(left, right, dims, preferred_element_type=jnp.float32)


def rim_kernel(raw_ref, weights_ref, out_ref):
    step = DECIM * LANES
    out_ref[:, :LANES] = product(raw_ref[:, : step + LANES], weights_ref[...])
    later = product(raw_ref[:, step : 2 * step + LANES], weights_ref[...])
    raw = pltpu.roll(raw_ref[:, :LANES].astype(jnp.float32), RIM % LANES, 1)
    lane = lax.broadcasted_iota(jnp.int32, raw.shape, 1)
    out_ref[:, LANES:] = jnp.where(lane < RIM % LANES, later, raw)


def trace_kernel(norm_ref, raw_ref, rim_ref, weights_ref, shift_ref, out_ref):
    channels = raw_ref.shape[0]
    step = DECIM * LANES
    own = raw_ref.shape[1] // step
    blocks = []
    for i in range(own - 1):
        blocks.append(product(raw_ref[:, i * step : i * step + step + LANES], weights_ref[...]))
    raw_rim = pltpu.roll(rim_ref[:, LANES:], LANES - RIM % LANES, 1).astype(jnp.bfloat16)
    blocks.append(
        product(raw_ref[:, (own - 1) * step :], weights_ref[:, :step])
        + product(raw_rim, weights_ref[:, step:])
    )
    blocks.append(rim_ref[...])
    squares = blocks[0] * blocks[0]
    for block in blocks[1:own]:
        squares = squares + block * block
    power = jnp.sum(squares, axis=1, keepdims=True)

    rows = jnp.concatenate(blocks, axis=1)
    shift = shift_ref[...]
    width = rows.shape[1]
    for bit in range(SHIFT_MAX.bit_length()):
        hop = 1 << bit
        moved = pltpu.roll(rows, width - hop, 1)
        rows = jnp.where((shift & hop) != 0, moved, rows)
    rows = rows[:, :WIDE]
    lane = lax.broadcasted_iota(jnp.int32, rows.shape, 1)
    rows = jnp.where(lane == WIDE - 1, power, rows)
    spare = GROUP - USED
    side = lax.broadcasted_iota(jnp.int32, (spare, WIDE), 0)
    side = jnp.where(side == 0, norm_ref[0], 0.0)
    for g in range(GROUPS):
        first, last = g * USED, min((g + 1) * USED, channels)
        pieces = [rows[first:last]]
        if last - first < USED:
            pieces.append(jnp.zeros((USED - last + first, WIDE), jnp.float32))
        out_ref[g] = jnp.concatenate(pieces + [side], axis=0)


def corr_kernel(
    panel_ref, first_ref, second_ref, trace_ref, root_ref, out_ref, mixed, panels, shifted
):
    chunks = panel_ref.shape[0] // LANES
    lags = out_ref.shape[-1]
    count = ROWS // PAIR

    @pl.when(pl.program_id(0) == 0)
    def _():
        for i in range(chunks):
            part = jnp.dot(
                first_ref[...], panel_ref[i * LANES : (i + 1) * LANES, :],
                preferred_element_type=jnp.float32,
            ).astype(jnp.bfloat16)
            for r in range(ROWS):
                mixed[r, i * SUB : (i + 1) * SUB, :] = part[r * SUB : (r + 1) * SUB, :]
        for r in range(ROWS):
            part = jnp.dot(
                second_ref[...], mixed[r], preferred_element_type=jnp.float32
            ).astype(jnp.bfloat16)
            a, h = divmod(r, PAIR)
            panels[a * LANES : (a + 1) * LANES, h * WIDE : (h + 1) * WIDE] = part

    pieces = trace_ref.shape[0]
    for t in range(pieces):
        trace = (trace_ref[t] / root_ref[...]).astype(jnp.bfloat16).astype(jnp.float32)
        for j in range(PAIR * SUB // 2):
            low = trace if j == 0 else pltpu.roll(trace, WIDE - 2 * j, 1)
            high = pltpu.roll(trace, WIDE - 2 * j - 1, 1)
            both = jnp.concatenate([low, high], axis=0).astype(jnp.bfloat16)
            shifted[j * 2 * GROUP : (j + 1) * 2 * GROUP, t * WIDE : (t + 1) * WIDE] = both
    sums = jnp.dot(panels[...], shifted[...], preferred_element_type=jnp.float32)
    for t in range(pieces):
        total = sums[:LANES, t * WIDE : t * WIDE + lags]
        for a in range(1, count):
            part = sums[a * LANES : (a + 1) * LANES, t * WIDE : (t + 1) * WIDE]
            total = total + pltpu.roll(part, WIDE - a * PAIR * SUB, 1)[:, :lags]
        for c in range(2):
            for x in range(2):
                g = c * 2 + x
                out_ref[c, x, t] = total[g * 32 : (g + 1) * 32, :]


def orders():
    first = np.zeros((LANES, LANES), np.float32)
    for src in range(SUB):
        for r in range(ROWS):
            first[r * SUB + src, src * ROWS + r] = 1
    second = np.zeros((LANES, LANES), np.float32)
    for zq in range(8):
        for y in range(4):
            for xl in range(2):
                for zp in range(2):
                    source = ((zq * 4 + y) * 2 + xl) * 2 + zp
                    x, c = divmod(y, 2)
                    target = (((c * 2 + x) * 2 + xl) * 8 + zq) * 2 + zp
                    second[target, source] = 1
    return jnp.asarray(first, jnp.bfloat16), jnp.asarray(second, jnp.bfloat16)


def whole(shape):
    return pl.BlockSpec(shape, lambda i: (0,) * len(shape))


def correlate(gathered, traces, root_power, lags):
    first, second = orders()
    depth = PAIR * SUB * GROUP
    flops = 2 * ROWS // PAIR * LANES * depth * WIDE * GROUPS
    return pl.pallas_call(
        corr_kernel,
        grid=(GROUPS // PIECES,),
        in_specs=[
            whole(gathered.shape),
            whole(first.shape),
            whole(second.shape),
            pl.BlockSpec((PIECES, GROUP, WIDE), lambda i: (i, 0, 0)),
            whole(root_power.shape),
        ],
        out_specs=pl.BlockSpec((2, 2, PIECES, 32, lags), lambda i: (0, 0, i, 0, 0)),
        out_shape=jax.ShapeDtypeStruct((2, 2, GROUPS, 32, lags), jnp.float32),
        scratch_shapes=[
            pltpu.VMEM((ROWS, LANES, WIDE), jnp.bfloat16),
            pltpu.VMEM((ROWS // PAIR * LANES, depth), jnp.bfloat16),
            pltpu.VMEM((depth, PIECES * WIDE), jnp.bfloat16),
        ],
        compiler_params=params(48),
        cost_estimate=pl.CostEstimate(flops=flops, bytes_accessed=4 << 20, transcendentals=0),
    )(gathered, first, second, traces, root_power)


def local(raw_traces, fir_taps, templates, start_offsets, channel_mask, station_shifts):
    channels, raw_len = raw_traces.shape
    lags = raw_len // DECIM
    blocks = lax.axis_size(BLK)
    weights = tap_matrix(fir_taps)
    rim = pl.pallas_call(
        rim_kernel,
        in_specs=[vmem()] * 2,
        out_specs=vmem(),
        out_shape=jax.ShapeDtypeStruct((channels, 2 * LANES), jnp.float32),
        compiler_params=params(32),
        cost_estimate=pl.CostEstimate(flops=128 << 20, bytes_accessed=2 << 20, transcendentals=0),
    )(raw_traces[:, : 2 * DECIM * LANES + LANES], weights)
    rim = from_next_block(rim)

    window = lax.dynamic_slice_in_dim(templates[0], start_offsets[0], TLEN, axis=1)
    panel = window * channel_mask[0].astype(jnp.bfloat16)[:, None]
    norm = jnp.sum(jnp.square(panel.astype(jnp.float32)))[None]
    padded = jnp.pad(panel, ((0, GROUPS * USED - channels), (0, 0)))
    padded = jnp.pad(padded.reshape(GROUPS, USED, TLEN), ((0, 0), (0, GROUP - USED), (0, 0)))
    message = padded.reshape(GROUPS, GROUP, ROWS, SUB).transpose(0, 2, 3, 1)
    message = message.reshape(GROUPS, 1, ROWS, SUB * GROUP)
    message = jnp.broadcast_to(message, (GROUPS, 2, ROWS, SUB * GROUP))
    message = message.reshape(2 * GROUPS, ROWS, SUB * GROUP)
    exchanged = lax.all_to_all(message, ("y", "xl", "zp"), 0, 0, tiled=True)
    norm = norm + lax.ppermute(norm, "core", [(0, 1), (1, 0)])
    norm = norm + lax.ppermute(norm, "xh", [(0, 1), (1, 0)])
    exchanged, rim, norm = lax.optimization_barrier((exchanged, rim, norm))
    gathered = lax.all_gather(exchanged, "zq", axis=0, tiled=True)
    gathered = gathered.reshape(blocks * ROWS, SUB * GROUP)

    traces = pl.pallas_call(
        trace_kernel,
        in_specs=[pl.BlockSpec(memory_space=pltpu.SMEM)] + [vmem()] * 4,
        out_specs=vmem(),
        out_shape=jax.ShapeDtypeStruct((GROUPS, GROUP, WIDE), jnp.float32),
        compiler_params=params(32),
        cost_estimate=pl.CostEstimate(flops=400 << 20, bytes_accessed=4 << 20, transcendentals=0),
    )(norm, raw_traces, rim, weights, jnp.repeat(station_shifts, 3)[:, None])
    traces = lax.all_to_all(traces, ("y", "xl"), 0, 0, tiled=True)

    powers = jnp.sum(traces[:, :, WIDE - 1], axis=0)
    norms = traces[:, USED, 0]
    facts = jnp.concatenate([powers, norms, jnp.zeros((LANES - GROUP - GROUPS,), jnp.float32)])
    along = lax.axis_size(("zq", "zp"))
    facts = jnp.broadcast_to(facts[None], (along, LANES))
    facts = lax.all_to_all(facts, ("zq", "zp"), 0, 0, tiled=True)
    powers = jnp.sum(facts[:, :GROUP], axis=0)
    root_power = jnp.sqrt(powers / (lags * blocks) + 1e-06)
    norms = facts[:, GROUP : GROUP + GROUPS].T.reshape(4, 2 * along)
    norms = lax.dynamic_index_in_dim(norms, lax.axis_index(("xh", "core")), 0, keepdims=False)

    sums = correlate(gathered, traces, root_power[:, None], lags)
    sums = jnp.sum(lax.all_to_all(sums, "core", 0, 0, tiled=True), axis=0)
    sums = sums.astype(jnp.bfloat16).reshape(2 * GROUPS, 32, lags)
    sums = lax.all_to_all(sums, ("xh", "y", "xl"), 0, 0, tiled=True)
    sums = jnp.sum(sums.astype(jnp.float32), axis=0)
    return sums / jnp.sqrt(norms + 1e-05)[:, None]


def solution(mesh):
    fine = Mesh(
        mesh.devices.reshape(2, 4, 2, 8, 2, 2), ("xh", "y", "xl", "zq", "zp", "core")
    )
    parts = ("xh", "core")
    return jax.shard_map(
        local,
        mesh=fine,
        in_specs=(P(parts, BLK), P(), P(BLK, parts, None), P(BLK), P(BLK, parts), P(parts)),
        out_specs=P(parts, BLK),
        check_vma=False,
    )
```

```python
import jax
import jax.numpy as jnp
import numpy as np
from jax import lax
from jax.experimental import pallas as pl
from jax.experimental.pallas import tpu as pltpu
from jax.sharding import Mesh, PartitionSpec as P

TLEN = 128
NTAP = 60
DECIM = 5
SHIFT_MAX = 64
LANES = 128
SUB = 16
ROWS = TLEN // SUB
PAIR = 2
WIDE = 640
GROUPS = 8
GROUP = 40
USED = 38
RIM = 192
PIECES = 2
BLK = ("y", "xl", "zq", "zp")


def vmem():
    return pl.BlockSpec(memory_space=pltpu.VMEM)


def params(mib):
    return pltpu.CompilerParams(vmem_limit_bytes=mib << 20)


def from_next_block(value):
    count = 128
    return lax.ppermute(value, BLK, [(i + 1, i) for i in range(count - 1)])


def tap_matrix(fir_taps):
    depth = DECIM * LANES + LANES
    pattern = jnp.concatenate([fir_taps, jnp.zeros((depth + DECIM - NTAP,), fir_taps.dtype)])
    flat = jnp.tile(pattern, LANES)[: LANES * depth]
    return flat.reshape(LANES, depth)


def product(left, right):
    dims = (((1,), (1,)), ((), ()))
    return lax.dot_general(left, right, dims, preferred_element_type=jnp.float32)


def rim_kernel(raw_ref, weights_ref, out_ref):
    step = DECIM * LANES
    out_ref[:, :LANES] = product(raw_ref[:, : step + LANES], weights_ref[...])
    later = product(raw_ref[:, step : 2 * step + LANES], weights_ref[...])
    raw = pltpu.roll(raw_ref[:, :LANES].astype(jnp.float32), RIM % LANES, 1)
    lane = lax.broadcasted_iota(jnp.int32, raw.shape, 1)
    out_ref[:, LANES:] = jnp.where(lane < RIM % LANES, later, raw)


def trace_kernel(norm_ref, raw_ref, rim_ref, weights_ref, shift_ref, out_ref):
    channels = raw_ref.shape[0]
    step = DECIM * LANES
    own = raw_ref.shape[1] // step
    blocks = []
    for i in range(own - 1):
        blocks.append(product(raw_ref[:, i * step : i * step + step + LANES], weights_ref[...]))
    raw_rim = pltpu.roll(rim_ref[:, LANES:], LANES - RIM % LANES, 1).astype(jnp.bfloat16)
    blocks.append(
        product(raw_ref[:, (own - 1) * step :], weights_ref[:, :step])
        + product(raw_rim, weights_ref[:, step:])
    )
    blocks.append(rim_ref[...])
    squares = blocks[0] * blocks[0]
    for block in blocks[1:own]:
        squares = squares + block * block
    power = jnp.sum(squares, axis=1, keepdims=True)

    rows = jnp.concatenate(blocks, axis=1)
    shift = shift_ref[...]
    width = rows.shape[1]
    for bit in range(SHIFT_MAX.bit_length()):
        hop = 1 << bit
        moved = pltpu.roll(rows, width - hop, 1)
        rows = jnp.where((shift & hop) != 0, moved, rows)
    rows = rows[:, :WIDE]
    lane = lax.broadcasted_iota(jnp.int32, rows.shape, 1)
    rows = jnp.where(lane == WIDE - 1, power, rows)
    spare = GROUP - USED
    side = lax.broadcasted_iota(jnp.int32, (spare, WIDE), 0)
    side = jnp.where(side == 0, norm_ref[0], 0.0)
    for g in range(GROUPS):
        first, last = g * USED, min((g + 1) * USED, channels)
        pieces = [rows[first:last]]
        if last - first < USED:
            pieces.append(jnp.zeros((USED - last + first, WIDE), jnp.float32))
        out_ref[g] = jnp.concatenate(pieces + [side], axis=0)


def corr_kernel(
    panel_ref, first_ref, second_ref, trace_ref, root_ref, out_ref, mixed, panels, shifted
):
    chunks = panel_ref.shape[0] // LANES
    lags = out_ref.shape[-1]
    count = ROWS // PAIR

    @pl.when(pl.program_id(0) == 0)
    def _():
        for i in range(chunks):
            part = jnp.dot(
                first_ref[...], panel_ref[i * LANES : (i + 1) * LANES, :],
                preferred_element_type=jnp.float32,
            ).astype(jnp.bfloat16)
            for r in range(ROWS):
                mixed[r, i * SUB : (i + 1) * SUB, :] = part[r * SUB : (r + 1) * SUB, :]
        for r in range(ROWS):
            part = jnp.dot(
                second_ref[...], mixed[r], preferred_element_type=jnp.float32
            ).astype(jnp.bfloat16)
            a, h = divmod(r, PAIR)
            panels[a * LANES : (a + 1) * LANES, h * WIDE : (h + 1) * WIDE] = part

    pieces = trace_ref.shape[0]
    for t in range(pieces):
        trace = (trace_ref[t] / root_ref[...]).astype(jnp.bfloat16).astype(jnp.float32)
        for j in range(PAIR * SUB // 2):
            low = trace if j == 0 else pltpu.roll(trace, WIDE - 2 * j, 1)
            high = pltpu.roll(trace, WIDE - 2 * j - 1, 1)
            both = jnp.concatenate([low, high], axis=0).astype(jnp.bfloat16)
            shifted[j * 2 * GROUP : (j + 1) * 2 * GROUP, t * WIDE : (t + 1) * WIDE] = both
    sums = jnp.dot(panels[...], shifted[...], preferred_element_type=jnp.float32)
    for t in range(pieces):
        total = sums[:LANES, t * WIDE : t * WIDE + lags]
        for a in range(1, count):
            part = sums[a * LANES : (a + 1) * LANES, t * WIDE : (t + 1) * WIDE]
            total = total + pltpu.roll(part, WIDE - a * PAIR * SUB, 1)[:, :lags]
        for c in range(2):
            for x in range(2):
                g = c * 2 + x
                out_ref[c, x, t] = total[g * 32 : (g + 1) * 32, :]


def orders():
    first = np.zeros((LANES, LANES), np.float32)
    for src in range(SUB):
        for r in range(ROWS):
            first[r * SUB + src, src * ROWS + r] = 1
    second = np.zeros((LANES, LANES), np.float32)
    for zq in range(8):
        for y in range(4):
            for xl in range(2):
                for zp in range(2):
                    source = ((zq * 4 + y) * 2 + xl) * 2 + zp
                    x, c = divmod(y, 2)
                    target = (((c * 2 + x) * 2 + xl) * 8 + zq) * 2 + zp
                    second[target, source] = 1
    return jnp.asarray(first, jnp.bfloat16), jnp.asarray(second, jnp.bfloat16)


def whole(shape):
    return pl.BlockSpec(shape, lambda i: (0,) * len(shape))


def correlate(gathered, traces, root_power, lags):
    first, second = orders()
    depth = PAIR * SUB * GROUP
    flops = 2 * ROWS // PAIR * LANES * depth * WIDE * GROUPS
    return pl.pallas_call(
        corr_kernel,
        grid=(GROUPS // PIECES,),
        in_specs=[
            whole(gathered.shape),
            whole(first.shape),
            whole(second.shape),
            pl.BlockSpec((PIECES, GROUP, WIDE), lambda i: (i, 0, 0)),
            whole(root_power.shape),
        ],
        out_specs=pl.BlockSpec((2, 2, PIECES, 32, lags), lambda i: (0, 0, i, 0, 0)),
        out_shape=jax.ShapeDtypeStruct((2, 2, GROUPS, 32, lags), jnp.float32),
        scratch_shapes=[
            pltpu.VMEM((ROWS, LANES, WIDE), jnp.bfloat16),
            pltpu.VMEM((ROWS // PAIR * LANES, depth), jnp.bfloat16),
            pltpu.VMEM((depth, PIECES * WIDE), jnp.bfloat16),
        ],
        compiler_params=params(48),
        cost_estimate=pl.CostEstimate(flops=flops, bytes_accessed=4 << 20, transcendentals=0),
    )(gathered, first, second, traces, root_power)


def local(raw_traces, fir_taps, templates, start_offsets, channel_mask, station_shifts):
    channels, raw_len = raw_traces.shape
    lags = raw_len // DECIM
    blocks = lax.axis_size(BLK)
    weights = tap_matrix(fir_taps)
    rim = pl.pallas_call(
        rim_kernel,
        in_specs=[vmem()] * 2,
        out_specs=vmem(),
        out_shape=jax.ShapeDtypeStruct((channels, 2 * LANES), jnp.float32),
        compiler_params=params(32),
        cost_estimate=pl.CostEstimate(flops=128 << 20, bytes_accessed=2 << 20, transcendentals=0),
    )(raw_traces[:, : 2 * DECIM * LANES + LANES], weights)
    rim = from_next_block(rim)

    window = lax.dynamic_slice_in_dim(templates[0], start_offsets[0], TLEN, axis=1)
    panel = window * channel_mask[0].astype(jnp.bfloat16)[:, None]
    norm = jnp.sum(jnp.square(panel.astype(jnp.float32)))[None]
    padded = jnp.pad(panel, ((0, GROUPS * USED - channels), (0, 0)))
    padded = jnp.pad(padded.reshape(GROUPS, USED, TLEN), ((0, 0), (0, GROUP - USED), (0, 0)))
    message = padded.reshape(GROUPS, GROUP, ROWS, SUB).transpose(0, 2, 3, 1)
    message = message.reshape(GROUPS, 1, ROWS, SUB * GROUP)
    message = jnp.broadcast_to(message, (GROUPS, 2, ROWS, SUB * GROUP))
    message = message.reshape(2 * GROUPS, ROWS, SUB * GROUP)
    exchanged = lax.all_to_all(message, ("y", "xl", "zp"), 0, 0, tiled=True)
    exchanged, rim = lax.optimization_barrier((exchanged, rim))
    gathered = lax.all_gather(exchanged, "zq", axis=0, tiled=True)
    gathered = gathered.reshape(blocks * ROWS, SUB * GROUP)

    traces = pl.pallas_call(
        trace_kernel,
        in_specs=[pl.BlockSpec(memory_space=pltpu.SMEM)] + [vmem()] * 4,
        out_specs=vmem(),
        out_shape=jax.ShapeDtypeStruct((GROUPS, GROUP, WIDE), jnp.float32),
        compiler_params=params(32),
        cost_estimate=pl.CostEstimate(flops=400 << 20, bytes_accessed=4 << 20, transcendentals=0),
    )(norm, raw_traces, rim, weights, jnp.repeat(station_shifts, 3)[:, None])
    traces = lax.all_to_all(traces, ("y", "xl"), 0, 0, tiled=True)

    powers = jnp.sum(traces[:, :, WIDE - 1], axis=0)
    norms = traces[:, USED, 0]
    facts = jnp.concatenate([powers, norms, jnp.zeros((LANES - GROUP - GROUPS,), jnp.float32)])
    along = lax.axis_size(("zq", "zp"))
    facts = jnp.broadcast_to(facts[None], (along, LANES))
    facts = lax.all_to_all(facts, ("zq", "zp"), 0, 0, tiled=True)
    powers = jnp.sum(facts[:, :GROUP], axis=0)
    root_power = jnp.sqrt(powers / (lags * blocks) + 1e-06)
    norms = facts[:, GROUP : GROUP + GROUPS].T.reshape(4, 1, 2 * along)
    norms = jnp.sum(lax.all_to_all(norms, ("xh", "core"), 0, 0, tiled=True), axis=(0, 1))
    root_power, norms = lax.optimization_barrier((root_power, norms))

    sums = correlate(gathered, traces, root_power[:, None], lags)
    sums = jnp.sum(lax.all_to_all(sums, "core", 0, 0, tiled=True), axis=0)
    sums = sums.astype(jnp.bfloat16).reshape(2 * GROUPS, 32, lags)
    sums = lax.all_to_all(sums, ("xh", "y", "xl"), 0, 0, tiled=True)
    sums = jnp.sum(sums.astype(jnp.float32), axis=0)
    return sums / jnp.sqrt(norms + 1e-05)[:, None]


def solution(mesh):
    fine = Mesh(
        mesh.devices.reshape(2, 4, 2, 8, 2, 2), ("xh", "y", "xl", "zq", "zp", "core")
    )
    parts = ("xh", "core")
    return jax.shard_map(
        local,
        mesh=fine,
        in_specs=(P(parts, BLK), P(), P(BLK, parts, None), P(BLK), P(BLK, parts), P(parts)),
        out_specs=P(parts, BLK),
        check_vma=False,
    )
```

```python
import jax
import jax.numpy as jnp
import numpy as np
from jax import lax
from jax.experimental import pallas as pl
from jax.experimental.pallas import tpu as pltpu
from jax.sharding import Mesh, PartitionSpec as P

TLEN = 128
NTAP = 60
DECIM = 5
SHIFT_MAX = 64
LANES = 128
SUB = 16
ROWS = TLEN // SUB
PAIR = 2
WIDE = 640
GROUPS = 8
GROUP = 40
USED = 38
RIM = 192
PIECES = 4
BLK = ("y", "xl", "zq", "zp")


def vmem():
    return pl.BlockSpec(memory_space=pltpu.VMEM)


def params(mib):
    return pltpu.CompilerParams(vmem_limit_bytes=mib << 20)


def from_next_block(value):
    count = 128
    return lax.ppermute(value, BLK, [(i + 1, i) for i in range(count - 1)])


def tap_matrix(fir_taps):
    depth = DECIM * LANES + LANES
    pattern = jnp.concatenate([fir_taps, jnp.zeros((depth + DECIM - NTAP,), fir_taps.dtype)])
    flat = jnp.tile(pattern, LANES)[: LANES * depth]
    return flat.reshape(LANES, depth)


def product(left, right):
    dims = (((1,), (1,)), ((), ()))
    return lax.dot_general(left, right, dims, preferred_element_type=jnp.float32)


def front_kernel(
    start_ref, template_ref, mask_ref, order_ref, raw_ref, weights_ref,
    message_ref, rim_ref, norm_ref,
):
    step = DECIM * LANES
    rim_ref[:, :LANES] = product(raw_ref[:, : step + LANES], weights_ref[...])
    later = product(raw_ref[:, step : 2 * step + LANES], weights_ref[...])
    raw = pltpu.roll(raw_ref[:, :LANES].astype(jnp.float32), RIM % LANES, 1)
    lane = lax.broadcasted_iota(jnp.int32, raw.shape, 1)
    rim_ref[:, LANES:] = jnp.where(lane < RIM % LANES, later, raw)

    stored = template_ref[0].astype(jnp.float32)
    channels, width = stored.shape
    window = pltpu.roll(stored, lax.rem(width - start_ref[0], width), 1)[:, :TLEN]
    rest = jnp.zeros((mask_ref.shape[1] - channels, TLEN), jnp.float32)
    panel = jnp.concatenate([window, rest], axis=0).T * mask_ref[...].astype(jnp.float32)
    norm = jnp.sum(jnp.sum(panel * panel, axis=0, keepdims=True), axis=1, keepdims=True)
    norm_ref[...] = jnp.broadcast_to(norm, norm_ref.shape)

    mixed = jnp.dot(
        order_ref[...], panel.astype(jnp.bfloat16), preferred_element_type=jnp.float32
    )
    lane = lax.broadcasted_iota(jnp.int32, (ROWS, WIDE), 1)
    empty = jnp.zeros((ROWS, WIDE), jnp.float32)
    messages = [empty] * GROUPS
    for s in range(SUB):
        row = mixed[s * ROWS : (s + 1) * ROWS]
        row = jnp.concatenate([row, empty[:, row.shape[1] :]], axis=1)
        place = (lane >= s * GROUP) & (lane < s * GROUP + USED)
        for g in range(GROUPS):
            hop = (s * GROUP - g * USED) % WIDE
            moved = row if hop == 0 else pltpu.roll(row, hop, 1)
            messages[g] = jnp.where(place, moved, messages[g])
    for g in range(GROUPS):
        message = messages[g].astype(jnp.bfloat16)
        message_ref[2 * g] = message
        message_ref[2 * g + 1] = message


def trace_kernel(norm_ref, raw_ref, rim_ref, weights_ref, shift_ref, out_ref):
    channels = raw_ref.shape[0]
    step = DECIM * LANES
    own = raw_ref.shape[1] // step
    blocks = []
    for i in range(own - 1):
        blocks.append(product(raw_ref[:, i * step : i * step + step + LANES], weights_ref[...]))
    raw_rim = pltpu.roll(rim_ref[:, LANES:], LANES - RIM % LANES, 1).astype(jnp.bfloat16)
    blocks.append(
        product(raw_ref[:, (own - 1) * step :], weights_ref[:, :step])
        + product(raw_rim, weights_ref[:, step:])
    )
    blocks.append(rim_ref[...])
    squares = blocks[0] * blocks[0]
    for block in blocks[1:own]:
        squares = squares + block * block
    power = jnp.sum(squares, axis=1, keepdims=True)

    rows = jnp.concatenate(blocks, axis=1)
    shift = shift_ref[...]
    width = rows.shape[1]
    for bit in range(SHIFT_MAX.bit_length()):
        hop = 1 << bit
        moved = pltpu.roll(rows, width - hop, 1)
        rows = jnp.where((shift & hop) != 0, moved, rows)
    rows = rows[:, :WIDE]
    lane = lax.broadcasted_iota(jnp.int32, rows.shape, 1)
    rows = jnp.where(lane == WIDE - 1, power, rows)
    spare = GROUP - USED
    side = lax.broadcasted_iota(jnp.int32, (spare, WIDE), 0)
    side = jnp.where(side == 0, jnp.broadcast_to(norm_ref[:, :1], side.shape), 0.0)
    for g in range(GROUPS):
        first, last = g * USED, min((g + 1) * USED, channels)
        pieces = [rows[first:last]]
        if last - first < USED:
            pieces.append(jnp.zeros((USED - last + first, WIDE), jnp.float32))
        out_ref[g] = jnp.concatenate(pieces + [side], axis=0)


def corr_kernel(
    panel_ref, first_ref, second_ref, trace_ref, root_ref, out_ref, mixed, panels, shifted
):
    chunks = panel_ref.shape[0] // LANES
    lags = out_ref.shape[-1]
    count = ROWS // PAIR

    @pl.when(pl.program_id(0) == 0)
    def _():
        for i in range(chunks):
            part = jnp.dot(
                first_ref[...], panel_ref[i * LANES : (i + 1) * LANES, :],
                preferred_element_type=jnp.float32,
            ).astype(jnp.bfloat16)
            for r in range(ROWS):
                mixed[r, i * SUB : (i + 1) * SUB, :] = part[r * SUB : (r + 1) * SUB, :]
        for r in range(ROWS):
            part = jnp.dot(
                second_ref[...], mixed[r], preferred_element_type=jnp.float32
            ).astype(jnp.bfloat16)
            a, h = divmod(r, PAIR)
            panels[a * LANES : (a + 1) * LANES, h * WIDE : (h + 1) * WIDE] = part

    pieces = trace_ref.shape[0]
    for t in range(pieces):
        trace = (trace_ref[t] / root_ref[...]).astype(jnp.bfloat16).astype(jnp.float32)
        for j in range(PAIR * SUB // 2):
            low = trace if j == 0 else pltpu.roll(trace, WIDE - 2 * j, 1)
            high = pltpu.roll(trace, WIDE - 2 * j - 1, 1)
            both = jnp.concatenate([low, high], axis=0).astype(jnp.bfloat16)
            shifted[j * 2 * GROUP : (j + 1) * 2 * GROUP, t * WIDE : (t + 1) * WIDE] = both
    sums = jnp.dot(panels[...], shifted[...], preferred_element_type=jnp.float32)
    for t in range(pieces):
        total = sums[:LANES, t * WIDE : t * WIDE + lags]
        for a in range(1, count):
            part = sums[a * LANES : (a + 1) * LANES, t * WIDE : (t + 1) * WIDE]
            total = total + pltpu.roll(part, WIDE - a * PAIR * SUB, 1)[:, :lags]
        for c in range(2):
            for x in range(2):
                g = c * 2 + x
                out_ref[c, x, t] = total[g * 32 : (g + 1) * 32, :]


def orders():
    first = np.zeros((LANES, LANES), np.float32)
    for src in range(SUB):
        for r in range(ROWS):
            first[r * SUB + src, src * ROWS + r] = 1
    second = np.zeros((LANES, LANES), np.float32)
    for zq in range(8):
        for y in range(4):
            for xl in range(2):
                for zp in range(2):
                    source = ((zq * 4 + y) * 2 + xl) * 2 + zp
                    x, c = divmod(y, 2)
                    target = (((c * 2 + x) * 2 + xl) * 8 + zq) * 2 + zp
                    second[target, source] = 1
    return jnp.asarray(first, jnp.bfloat16), jnp.asarray(second, jnp.bfloat16)


def whole(shape):
    return pl.BlockSpec(shape, lambda i: (0,) * len(shape))


def correlate(gathered, traces, root_power, lags):
    first, second = orders()
    depth = PAIR * SUB * GROUP
    flops = 2 * ROWS // PAIR * LANES * depth * WIDE * GROUPS
    return pl.pallas_call(
        corr_kernel,
        grid=(GROUPS // PIECES,),
        in_specs=[
            whole(gathered.shape),
            whole(first.shape),
            whole(second.shape),
            pl.BlockSpec((PIECES, GROUP, WIDE), lambda i: (i, 0, 0)),
            whole(root_power.shape),
        ],
        out_specs=pl.BlockSpec((2, 2, PIECES, 32, lags), lambda i: (0, 0, i, 0, 0)),
        out_shape=jax.ShapeDtypeStruct((2, 2, GROUPS, 32, lags), jnp.float32),
        scratch_shapes=[
            pltpu.VMEM((ROWS, LANES, WIDE), jnp.bfloat16),
            pltpu.VMEM((ROWS // PAIR * LANES, depth), jnp.bfloat16),
            pltpu.VMEM((depth, PIECES * WIDE), jnp.bfloat16),
        ],
        compiler_params=params(48),
        cost_estimate=pl.CostEstimate(flops=flops, bytes_accessed=4 << 20, transcendentals=0),
    )(gathered, first, second, traces, root_power)


def local(raw_traces, fir_taps, templates, start_offsets, channel_mask, station_shifts):
    channels, raw_len = raw_traces.shape
    lags = raw_len // DECIM
    blocks = lax.axis_size(BLK)
    weights = tap_matrix(fir_taps)
    order = np.zeros((TLEN, TLEN), np.float32)
    for r in range(ROWS):
        for s in range(SUB):
            order[s * ROWS + r, r * SUB + s] = 1
    message, rim, norm = pl.pallas_call(
        front_kernel,
        in_specs=[pl.BlockSpec(memory_space=pltpu.SMEM)] + [vmem()] * 5,
        out_specs=[vmem()] * 3,
        out_shape=[
            jax.ShapeDtypeStruct((2 * GROUPS, ROWS, WIDE), jnp.bfloat16),
            jax.ShapeDtypeStruct((channels, 2 * LANES), jnp.float32),
            jax.ShapeDtypeStruct((1, LANES), jnp.float32),
        ],
        compiler_params=params(32),
        cost_estimate=pl.CostEstimate(flops=128 << 20, bytes_accessed=2 << 20, transcendentals=0),
    )(
        start_offsets, templates, jnp.pad(channel_mask, ((0, 0), (0, -channels % LANES))),
        jnp.asarray(order, jnp.bfloat16), raw_traces[:, : 2 * DECIM * LANES + LANES], weights,
    )
    rim = from_next_block(rim)
    exchanged = lax.all_to_all(message, ("y", "xl", "zp"), 0, 0, tiled=True)
    exchanged, rim = lax.optimization_barrier((exchanged, rim))
    gathered = lax.all_gather(exchanged, "zq", axis=0, tiled=True)
    gathered = gathered.reshape(blocks * ROWS, SUB * GROUP)

    traces = pl.pallas_call(
        trace_kernel,
        in_specs=[vmem()] * 5,
        out_specs=vmem(),
        out_shape=jax.ShapeDtypeStruct((GROUPS, GROUP, WIDE), jnp.float32),
        compiler_params=params(32),
        cost_estimate=pl.CostEstimate(flops=400 << 20, bytes_accessed=4 << 20, transcendentals=0),
    )(norm, raw_traces, rim, weights, jnp.repeat(station_shifts, 3)[:, None])
    traces = lax.all_to_all(traces, ("y", "xl"), 0, 0, tiled=True)

    powers = jnp.sum(traces[:, :, WIDE - 1], axis=0)
    norms = traces[:, USED, 0]
    facts = jnp.concatenate([powers, norms, jnp.zeros((LANES - GROUP - GROUPS,), jnp.float32)])
    along = lax.axis_size(("zq", "zp"))
    facts = jnp.broadcast_to(facts[None], (along, LANES))
    facts = lax.all_to_all(facts, ("zq", "zp"), 0, 0, tiled=True)
    powers = jnp.sum(facts[:, :GROUP], axis=0)
    root_power = jnp.sqrt(powers / (lags * blocks) + 1e-06)
    norms = facts[:, GROUP : GROUP + GROUPS].T.reshape(4, 1, 2 * along)
    norms = jnp.sum(lax.all_to_all(norms, ("xh", "core"), 0, 0, tiled=True), axis=(0, 1))
    root_power, norms = lax.optimization_barrier((root_power, norms))

    sums = correlate(gathered, traces, root_power[:, None], lags)
    sums = jnp.sum(lax.all_to_all(sums, "core", 0, 0, tiled=True), axis=0)
    sums = sums.astype(jnp.bfloat16).reshape(2 * GROUPS, 32, lags)
    sums = lax.all_to_all(sums, ("xh", "y", "xl"), 0, 0, tiled=True)
    sums = jnp.sum(sums.astype(jnp.float32), axis=0)
    return sums / jnp.sqrt(norms + 1e-05)[:, None]


def solution(mesh):
    fine = Mesh(
        mesh.devices.reshape(2, 4, 2, 8, 2, 2), ("xh", "y", "xl", "zq", "zp", "core")
    )
    parts = ("xh", "core")
    return jax.shard_map(
        local,
        mesh=fine,
        in_specs=(P(parts, BLK), P(), P(BLK, parts, None), P(BLK), P(BLK, parts), P(parts)),
        out_specs=P(parts, BLK),
        check_vma=False,
    )
```

```python
import jax
import jax.numpy as jnp
import numpy as np
from jax import lax
from jax.experimental import pallas as pl
from jax.experimental.pallas import tpu as pltpu
from jax.sharding import Mesh, PartitionSpec as P

TLEN = 128
NTAP = 60
DECIM = 5
SHIFT_MAX = 64
LANES = 128
SUB = 16
ROWS = TLEN // SUB
PAIR = 2
WIDE = 640
GROUPS = 8
GROUP = 40
USED = 38
RIM = 192
PIECES = 4
BLK = ("y", "xl", "zq", "zp")


def vmem():
    return pl.BlockSpec(memory_space=pltpu.VMEM)


def params(mib):
    return pltpu.CompilerParams(vmem_limit_bytes=mib << 20)


def from_next_block(value):
    count = 128
    return lax.ppermute(value, BLK, [(i + 1, i) for i in range(count - 1)])


def product(left, right):
    dims = (((1,), (1,)), ((), ()))
    return lax.dot_general(left, right, dims, preferred_element_type=jnp.float32)


def front_kernel(
    start_ref, taps_ref, template_ref, mask_ref, order_ref, raw_ref,
    message_ref, rim_ref, norm_ref, weights_ref,
):
    step = DECIM * LANES
    taps = jnp.broadcast_to(taps_ref[...].astype(jnp.float32), (8, LANES))
    taps = pltpu.roll(taps, 0, 1, stride=DECIM, stride_axis=0)
    taps = jnp.concatenate([taps, jnp.zeros((8, step), jnp.float32)], axis=1)
    tiles = [taps] + [pltpu.roll(taps, 8 * DECIM * i, 1) for i in range(1, LANES // 8)]
    weights_ref[...] = jnp.concatenate(tiles, axis=0).astype(jnp.bfloat16)
    rim_ref[:, :LANES] = product(raw_ref[:, : step + LANES], weights_ref[...])
    later = product(raw_ref[:, step : 2 * step + LANES], weights_ref[...])
    raw = pltpu.roll(raw_ref[:, :LANES].astype(jnp.float32), RIM % LANES, 1)
    lane = lax.broadcasted_iota(jnp.int32, raw.shape, 1)
    rim_ref[:, LANES:] = jnp.where(lane < RIM % LANES, later, raw)

    stored = template_ref[0].astype(jnp.float32)
    channels, width = stored.shape
    window = pltpu.roll(stored, lax.rem(width - start_ref[0], width), 1)[:, :TLEN]
    rest = jnp.zeros((mask_ref.shape[1] - channels, TLEN), jnp.float32)
    panel = jnp.concatenate([window, rest], axis=0).T * mask_ref[...].astype(jnp.float32)
    norm = jnp.sum(jnp.sum(panel * panel, axis=0, keepdims=True), axis=1, keepdims=True)
    norm_ref[...] = jnp.broadcast_to(norm, norm_ref.shape)

    mixed = jnp.dot(
        order_ref[...], panel.astype(jnp.bfloat16), preferred_element_type=jnp.float32
    )
    lane = lax.broadcasted_iota(jnp.int32, (ROWS, WIDE), 1)
    empty = jnp.zeros((ROWS, WIDE), jnp.float32)
    messages = [empty] * GROUPS
    for s in range(SUB):
        row = mixed[s * ROWS : (s + 1) * ROWS]
        row = jnp.concatenate([row, empty[:, row.shape[1] :]], axis=1)
        place = (lane >= s * GROUP) & (lane < s * GROUP + USED)
        for g in range(GROUPS):
            hop = (s * GROUP - g * USED) % WIDE
            moved = row if hop == 0 else pltpu.roll(row, hop, 1)
            messages[g] = jnp.where(place, moved, messages[g])
    for g in range(GROUPS):
        message = messages[g].astype(jnp.bfloat16)
        message_ref[2 * g] = message
        message_ref[2 * g + 1] = message


def trace_kernel(norm_ref, raw_ref, rim_ref, weights_ref, shift_ref, out_ref):
    channels = raw_ref.shape[0]
    step = DECIM * LANES
    own = raw_ref.shape[1] // step
    blocks = []
    for i in range(own - 1):
        blocks.append(product(raw_ref[:, i * step : i * step + step + LANES], weights_ref[...]))
    raw_rim = pltpu.roll(rim_ref[:, LANES:], LANES - RIM % LANES, 1).astype(jnp.bfloat16)
    blocks.append(
        product(raw_ref[:, (own - 1) * step :], weights_ref[:, :step])
        + product(raw_rim, weights_ref[:, step:])
    )
    blocks.append(rim_ref[...])
    squares = blocks[0] * blocks[0]
    for block in blocks[1:own]:
        squares = squares + block * block
    power = jnp.sum(squares, axis=1, keepdims=True)

    rows = jnp.concatenate(blocks, axis=1)
    shift = shift_ref[...]
    width = rows.shape[1]
    for bit in range(SHIFT_MAX.bit_length()):
        hop = 1 << bit
        moved = pltpu.roll(rows, width - hop, 1)
        rows = jnp.where((shift & hop) != 0, moved, rows)
    rows = rows[:, :WIDE]
    lane = lax.broadcasted_iota(jnp.int32, rows.shape, 1)
    rows = jnp.where(lane == WIDE - 1, power, rows)
    spare = GROUP - USED
    side = lax.broadcasted_iota(jnp.int32, (spare, WIDE), 0)
    side = jnp.where(side == 0, jnp.broadcast_to(norm_ref[:, :1], side.shape), 0.0)
    for g in range(GROUPS):
        first, last = g * USED, min((g + 1) * USED, channels)
        pieces = [rows[first:last]]
        if last - first < USED:
            pieces.append(jnp.zeros((USED - last + first, WIDE), jnp.float32))
        out_ref[g] = jnp.concatenate(pieces + [side], axis=0)


def corr_kernel(
    panel_ref, first_ref, second_ref, trace_ref, root_ref, out_ref, mixed, panels, shifted
):
    chunks = panel_ref.shape[0] // LANES
    lags = out_ref.shape[-1]
    count = ROWS // PAIR

    @pl.when(pl.program_id(0) == 0)
    def _():
        for i in range(chunks):
            part = jnp.dot(
                first_ref[...], panel_ref[i * LANES : (i + 1) * LANES, :],
                preferred_element_type=jnp.float32,
            ).astype(jnp.bfloat16)
            for r in range(ROWS):
                mixed[r, i * SUB : (i + 1) * SUB, :] = part[r * SUB : (r + 1) * SUB, :]
        for r in range(ROWS):
            part = jnp.dot(
                second_ref[...], mixed[r], preferred_element_type=jnp.float32
            ).astype(jnp.bfloat16)
            a, h = divmod(r, PAIR)
            panels[a * LANES : (a + 1) * LANES, h * WIDE : (h + 1) * WIDE] = part

    pieces = trace_ref.shape[0]
    for t in range(pieces):
        trace = (trace_ref[t] / root_ref[...]).astype(jnp.bfloat16).astype(jnp.float32)
        for j in range(PAIR * SUB // 2):
            low = trace if j == 0 else pltpu.roll(trace, WIDE - 2 * j, 1)
            high = pltpu.roll(trace, WIDE - 2 * j - 1, 1)
            both = jnp.concatenate([low, high], axis=0).astype(jnp.bfloat16)
            shifted[j * 2 * GROUP : (j + 1) * 2 * GROUP, t * WIDE : (t + 1) * WIDE] = both
    sums = jnp.dot(panels[...], shifted[...], preferred_element_type=jnp.float32)
    for t in range(pieces):
        total = sums[:LANES, t * WIDE : t * WIDE + lags]
        for a in range(1, count):
            part = sums[a * LANES : (a + 1) * LANES, t * WIDE : (t + 1) * WIDE]
            total = total + pltpu.roll(part, WIDE - a * PAIR * SUB, 1)[:, :lags]
        for c in range(2):
            for x in range(2):
                g = c * 2 + x
                out_ref[c, x, t] = total[g * 32 : (g + 1) * 32, :]


def orders():
    first = np.zeros((LANES, LANES), np.float32)
    for src in range(SUB):
        for r in range(ROWS):
            first[r * SUB + src, src * ROWS + r] = 1
    second = np.zeros((LANES, LANES), np.float32)
    for zq in range(8):
        for y in range(4):
            for xl in range(2):
                for zp in range(2):
                    source = ((zq * 4 + y) * 2 + xl) * 2 + zp
                    x, c = divmod(y, 2)
                    target = (((c * 2 + x) * 2 + xl) * 8 + zq) * 2 + zp
                    second[target, source] = 1
    return jnp.asarray(first, jnp.bfloat16), jnp.asarray(second, jnp.bfloat16)


def whole(shape):
    return pl.BlockSpec(shape, lambda i: (0,) * len(shape))


def correlate(gathered, traces, root_power, lags):
    first, second = orders()
    depth = PAIR * SUB * GROUP
    flops = 2 * ROWS // PAIR * LANES * depth * WIDE * GROUPS
    return pl.pallas_call(
        corr_kernel,
        grid=(GROUPS // PIECES,),
        in_specs=[
            whole(gathered.shape),
            whole(first.shape),
            whole(second.shape),
            pl.BlockSpec((PIECES, GROUP, WIDE), lambda i: (i, 0, 0)),
            whole(root_power.shape),
        ],
        out_specs=pl.BlockSpec((2, 2, PIECES, 32, lags), lambda i: (0, 0, i, 0, 0)),
        out_shape=jax.ShapeDtypeStruct((2, 2, GROUPS, 32, lags), jnp.float32),
        scratch_shapes=[
            pltpu.VMEM((ROWS, LANES, WIDE), jnp.bfloat16),
            pltpu.VMEM((ROWS // PAIR * LANES, depth), jnp.bfloat16),
            pltpu.VMEM((depth, PIECES * WIDE), jnp.bfloat16),
        ],
        compiler_params=params(48),
        cost_estimate=pl.CostEstimate(flops=flops, bytes_accessed=4 << 20, transcendentals=0),
    )(gathered, first, second, traces, root_power)


def local(raw_traces, fir_taps, templates, start_offsets, channel_mask, station_shifts):
    channels, raw_len = raw_traces.shape
    lags = raw_len // DECIM
    blocks = lax.axis_size(BLK)
    order = np.zeros((TLEN, TLEN), np.float32)
    for r in range(ROWS):
        for s in range(SUB):
            order[s * ROWS + r, r * SUB + s] = 1
    depth = DECIM * LANES + LANES
    taps = jnp.pad(fir_taps, (0, LANES - NTAP))[None]
    mask = jnp.pad(channel_mask, ((0, 0), (0, -channels % LANES)))
    near = (channels, 2 * DECIM * LANES + LANES)
    message, rim, norm, weights = pl.pallas_call(
        front_kernel,
        grid=(1,),
        in_specs=[
            pl.BlockSpec(memory_space=pltpu.SMEM),
            whole(taps.shape),
            whole(templates.shape),
            whole(mask.shape),
            whole(order.shape),
            whole(near),
        ],
        out_specs=[
            whole((2 * GROUPS, ROWS, WIDE)),
            whole((channels, 2 * LANES)),
            whole((1, LANES)),
            whole((LANES, depth)),
        ],
        out_shape=[
            jax.ShapeDtypeStruct((2 * GROUPS, ROWS, WIDE), jnp.bfloat16),
            jax.ShapeDtypeStruct((channels, 2 * LANES), jnp.float32),
            jax.ShapeDtypeStruct((1, LANES), jnp.float32),
            jax.ShapeDtypeStruct((LANES, depth), jnp.bfloat16),
        ],
        compiler_params=params(32),
        cost_estimate=pl.CostEstimate(flops=128 << 20, bytes_accessed=2 << 20, transcendentals=0),
    )(start_offsets, taps, templates, mask, jnp.asarray(order, jnp.bfloat16), raw_traces)
    rim = from_next_block(rim)
    exchanged = lax.all_to_all(message, ("y", "xl", "zp"), 0, 0, tiled=True)
    exchanged, rim = lax.optimization_barrier((exchanged, rim))
    gathered = lax.all_gather(exchanged, "zq", axis=0, tiled=True)
    gathered = gathered.reshape(blocks * ROWS, SUB * GROUP)

    traces = pl.pallas_call(
        trace_kernel,
        in_specs=[vmem()] * 5,
        out_specs=vmem(),
        out_shape=jax.ShapeDtypeStruct((GROUPS, GROUP, WIDE), jnp.float32),
        compiler_params=params(32),
        cost_estimate=pl.CostEstimate(flops=400 << 20, bytes_accessed=4 << 20, transcendentals=0),
    )(norm, raw_traces, rim, weights, jnp.repeat(station_shifts, 3)[:, None])
    traces = lax.all_to_all(traces, ("y", "xl"), 0, 0, tiled=True)

    powers = jnp.sum(traces[:, :, WIDE - 1], axis=0)
    norms = traces[:, USED, 0]
    facts = jnp.concatenate([powers, norms, jnp.zeros((LANES - GROUP - GROUPS,), jnp.float32)])
    along = lax.axis_size(("zq", "zp"))
    facts = jnp.broadcast_to(facts[None], (along, LANES))
    facts = lax.all_to_all(facts, ("zq", "zp"), 0, 0, tiled=True)
    powers = jnp.sum(facts[:, :GROUP], axis=0)
    root_power = jnp.sqrt(powers / (lags * blocks) + 1e-06)
    norms = facts[:, GROUP : GROUP + GROUPS].T.reshape(4, 1, 2 * along)
    norms = jnp.sum(lax.all_to_all(norms, ("xh", "core"), 0, 0, tiled=True), axis=(0, 1))
    root_power, norms = lax.optimization_barrier((root_power, norms))

    sums = correlate(gathered, traces, root_power[:, None], lags)
    sums = jnp.sum(lax.all_to_all(sums, "core", 0, 0, tiled=True), axis=0)
    sums = sums.astype(jnp.bfloat16).reshape(2 * GROUPS, 32, lags)
    sums = lax.all_to_all(sums, ("xh", "y", "xl"), 0, 0, tiled=True)
    sums = jnp.sum(sums.astype(jnp.float32), axis=0)
    return sums / jnp.sqrt(norms + 1e-05)[:, None]


def solution(mesh):
    fine = Mesh(
        mesh.devices.reshape(2, 4, 2, 8, 2, 2), ("xh", "y", "xl", "zq", "zp", "core")
    )
    parts = ("xh", "core")
    return jax.shard_map(
        local,
        mesh=fine,
        in_specs=(P(parts, BLK), P(), P(BLK, parts, None), P(BLK), P(BLK, parts), P(parts)),
        out_specs=P(parts, BLK),
        check_vma=False,
    )
```

```python
import jax
import jax.numpy as jnp
import numpy as np
from jax import lax
from jax.experimental import pallas as pl
from jax.experimental.pallas import tpu as pltpu
from jax.sharding import Mesh, PartitionSpec as P

TLEN = 128
NTAP = 60
DECIM = 5
SHIFT_MAX = 64
LANES = 128
SUB = 16
ROWS = TLEN // SUB
PAIR = 2
WIDE = 640
GROUPS = 8
GROUP = 40
USED = 38
RIM = 192
PIECES = 4
BLK = ("y", "xl", "zq", "zp")


def vmem():
    return pl.BlockSpec(memory_space=pltpu.VMEM)


def params(mib):
    return pltpu.CompilerParams(vmem_limit_bytes=mib << 20)


def from_next_block(value):
    count = 128
    return lax.ppermute(value, BLK, [(i + 1, i) for i in range(count - 1)])


def tap_matrix(fir_taps):
    depth = DECIM * LANES + LANES
    pattern = jnp.concatenate([fir_taps, jnp.zeros((depth + DECIM - NTAP,), fir_taps.dtype)])
    flat = jnp.tile(pattern, LANES)[: LANES * depth]
    return flat.reshape(LANES, depth)


def product(left, right):
    dims = (((1,), (1,)), ((), ()))
    return lax.dot_general(left, right, dims, preferred_element_type=jnp.float32)


def front_kernel(
    start_ref, template_ref, mask_ref, order_ref, raw_ref, weights_ref,
    message_ref, rim_ref, norm_ref,
):
    step = DECIM * LANES
    rim_ref[:, :LANES] = product(raw_ref[:, : step + LANES], weights_ref[...])
    later = product(raw_ref[:, step : 2 * step + LANES], weights_ref[...])
    raw = pltpu.roll(raw_ref[:, :LANES].astype(jnp.float32), RIM % LANES, 1)
    lane = lax.broadcasted_iota(jnp.int32, raw.shape, 1)
    rim_ref[:, LANES:] = jnp.where(lane < RIM % LANES, later, raw)

    stored = template_ref[0].astype(jnp.float32)
    channels, width = stored.shape
    window = pltpu.roll(stored, lax.rem(width - start_ref[0], width), 1)[:, :TLEN]
    rest = jnp.zeros((mask_ref.shape[1] - channels, TLEN), jnp.float32)
    panel = jnp.concatenate([window, rest], axis=0).T * mask_ref[...].astype(jnp.float32)
    norm = jnp.sum(jnp.sum(panel * panel, axis=0, keepdims=True), axis=1, keepdims=True)
    norm_ref[...] = jnp.broadcast_to(norm, norm_ref.shape)

    mixed = jnp.dot(
        order_ref[...], panel.astype(jnp.bfloat16), preferred_element_type=jnp.float32
    )
    lane = lax.broadcasted_iota(jnp.int32, (ROWS, WIDE), 1)
    empty = jnp.zeros((ROWS, WIDE), jnp.float32)
    messages = [empty] * GROUPS
    for s in range(SUB):
        row = mixed[s * ROWS : (s + 1) * ROWS]
        row = jnp.concatenate([row, empty[:, row.shape[1] :]], axis=1)
        place = (lane >= s * GROUP) & (lane < s * GROUP + USED)
        for g in range(GROUPS):
            hop = (s * GROUP - g * USED) % WIDE
            moved = row if hop == 0 else pltpu.roll(row, hop, 1)
            messages[g] = jnp.where(place, moved, messages[g])
    for g in range(GROUPS):
        message = messages[g].astype(jnp.bfloat16)
        message_ref[2 * g] = message
        message_ref[2 * g + 1] = message


def trace_kernel(norm_ref, raw_ref, rim_ref, weights_ref, shift_ref, out_ref):
    channels = raw_ref.shape[0]
    step = DECIM * LANES
    own = raw_ref.shape[1] // step
    blocks = []
    for i in range(own - 1):
        blocks.append(product(raw_ref[:, i * step : i * step + step + LANES], weights_ref[...]))
    raw_rim = pltpu.roll(rim_ref[:, LANES:], LANES - RIM % LANES, 1).astype(jnp.bfloat16)
    blocks.append(
        product(raw_ref[:, (own - 1) * step :], weights_ref[:, :step])
        + product(raw_rim, weights_ref[:, step:])
    )
    blocks.append(rim_ref[...])
    squares = blocks[0] * blocks[0]
    for block in blocks[1:own]:
        squares = squares + block * block
    power = jnp.sum(squares, axis=1, keepdims=True)

    rows = jnp.concatenate(blocks, axis=1)
    shift = shift_ref[...]
    width = rows.shape[1]
    for bit in range(SHIFT_MAX.bit_length()):
        hop = 1 << bit
        moved = pltpu.roll(rows, width - hop, 1)
        rows = jnp.where((shift & hop) != 0, moved, rows)
    rows = rows[:, :WIDE]
    lane = lax.broadcasted_iota(jnp.int32, rows.shape, 1)
    rows = jnp.where(lane == WIDE - 1, power, rows)
    spare = GROUP - USED
    side = lax.broadcasted_iota(jnp.int32, (spare, WIDE), 0)
    side = jnp.where(side == 0, jnp.broadcast_to(norm_ref[:, :1], side.shape), 0.0)
    for g in range(GROUPS):
        first, last = g * USED, min((g + 1) * USED, channels)
        pieces = [rows[first:last]]
        if last - first < USED:
            pieces.append(jnp.zeros((USED - last + first, WIDE), jnp.float32))
        out_ref[g] = jnp.concatenate(pieces + [side], axis=0)


def corr_kernel(
    panel_ref, first_ref, second_ref, trace_ref, root_ref, out_ref, mixed, panels, shifted
):
    chunks = panel_ref.shape[0] // LANES
    lags = out_ref.shape[-1]
    count = ROWS // PAIR

    @pl.when(pl.program_id(0) == 0)
    def _():
        for i in range(chunks):
            part = jnp.dot(
                first_ref[...], panel_ref[i * LANES : (i + 1) * LANES, :],
                preferred_element_type=jnp.float32,
            ).astype(jnp.bfloat16)
            for r in range(ROWS):
                mixed[r, i * SUB : (i + 1) * SUB, :] = part[r * SUB : (r + 1) * SUB, :]
        for r in range(ROWS):
            part = jnp.dot(
                second_ref[...], mixed[r], preferred_element_type=jnp.float32
            ).astype(jnp.bfloat16)
            a, h = divmod(r, PAIR)
            panels[a * LANES : (a + 1) * LANES, h * WIDE : (h + 1) * WIDE] = part

    pieces = trace_ref.shape[0]
    for t in range(pieces):
        trace = (trace_ref[t] / root_ref[...]).astype(jnp.bfloat16).astype(jnp.float32)
        for j in range(PAIR * SUB // 2):
            low = trace if j == 0 else pltpu.roll(trace, WIDE - 2 * j, 1)
            high = pltpu.roll(trace, WIDE - 2 * j - 1, 1)
            both = jnp.concatenate([low, high], axis=0).astype(jnp.bfloat16)
            shifted[j * 2 * GROUP : (j + 1) * 2 * GROUP, t * WIDE : (t + 1) * WIDE] = both
    sums = jnp.dot(panels[...], shifted[...], preferred_element_type=jnp.float32)
    for t in range(pieces):
        total = sums[:LANES, t * WIDE : t * WIDE + lags]
        for a in range(1, count):
            part = sums[a * LANES : (a + 1) * LANES, t * WIDE : (t + 1) * WIDE]
            total = total + pltpu.roll(part, WIDE - a * PAIR * SUB, 1)[:, :lags]
        for c in range(2):
            for x in range(2):
                g = c * 2 + x
                out_ref[c, x, t] = total[g * 32 : (g + 1) * 32, :].astype(jnp.bfloat16)


def orders():
    first = np.zeros((LANES, LANES), np.float32)
    for src in range(SUB):
        for r in range(ROWS):
            first[r * SUB + src, src * ROWS + r] = 1
    second = np.zeros((LANES, LANES), np.float32)
    for zq in range(8):
        for y in range(4):
            for xl in range(2):
                for zp in range(2):
                    source = ((zq * 4 + y) * 2 + xl) * 2 + zp
                    x, c = divmod(y, 2)
                    target = (((c * 2 + x) * 2 + xl) * 8 + zq) * 2 + zp
                    second[target, source] = 1
    return jnp.asarray(first, jnp.bfloat16), jnp.asarray(second, jnp.bfloat16)


def whole(shape):
    return pl.BlockSpec(shape, lambda i: (0,) * len(shape))


def correlate(gathered, traces, root_power, lags):
    first, second = orders()
    depth = PAIR * SUB * GROUP
    flops = 2 * ROWS // PAIR * LANES * depth * WIDE * GROUPS
    return pl.pallas_call(
        corr_kernel,
        grid=(GROUPS // PIECES,),
        in_specs=[
            whole(gathered.shape),
            whole(first.shape),
            whole(second.shape),
            pl.BlockSpec((PIECES, GROUP, WIDE), lambda i: (i, 0, 0)),
            whole(root_power.shape),
        ],
        out_specs=pl.BlockSpec((2, 2, PIECES, 32, lags), lambda i: (0, 0, i, 0, 0)),
        out_shape=jax.ShapeDtypeStruct((2, 2, GROUPS, 32, lags), jnp.bfloat16),
        scratch_shapes=[
            pltpu.VMEM((ROWS, LANES, WIDE), jnp.bfloat16),
            pltpu.VMEM((ROWS // PAIR * LANES, depth), jnp.bfloat16),
            pltpu.VMEM((depth, PIECES * WIDE), jnp.bfloat16),
        ],
        compiler_params=params(48),
        cost_estimate=pl.CostEstimate(flops=flops, bytes_accessed=4 << 20, transcendentals=0),
    )(gathered, first, second, traces, root_power)


def local(raw_traces, fir_taps, templates, start_offsets, channel_mask, station_shifts):
    channels, raw_len = raw_traces.shape
    lags = raw_len // DECIM
    blocks = lax.axis_size(BLK)
    weights = tap_matrix(fir_taps)
    order = np.zeros((TLEN, TLEN), np.float32)
    for r in range(ROWS):
        for s in range(SUB):
            order[s * ROWS + r, r * SUB + s] = 1
    message, rim, norm = pl.pallas_call(
        front_kernel,
        in_specs=[pl.BlockSpec(memory_space=pltpu.SMEM)] + [vmem()] * 5,
        out_specs=[vmem()] * 3,
        out_shape=[
            jax.ShapeDtypeStruct((2 * GROUPS, ROWS, WIDE), jnp.bfloat16),
            jax.ShapeDtypeStruct((channels, 2 * LANES), jnp.float32),
            jax.ShapeDtypeStruct((1, LANES), jnp.float32),
        ],
        compiler_params=params(32),
        cost_estimate=pl.CostEstimate(flops=128 << 20, bytes_accessed=2 << 20, transcendentals=0),
    )(
        start_offsets, templates, jnp.pad(channel_mask, ((0, 0), (0, -channels % LANES))),
        jnp.asarray(order, jnp.bfloat16), raw_traces[:, : 2 * DECIM * LANES + LANES], weights,
    )
    rim = from_next_block(rim)
    exchanged = lax.all_to_all(message, ("y", "xl", "zp"), 0, 0, tiled=True)
    exchanged, rim = lax.optimization_barrier((exchanged, rim))
    gathered = lax.all_gather(exchanged, "zq", axis=0, tiled=True)
    gathered = gathered.reshape(blocks * ROWS, SUB * GROUP)

    traces = pl.pallas_call(
        trace_kernel,
        in_specs=[vmem()] * 5,
        out_specs=vmem(),
        out_shape=jax.ShapeDtypeStruct((GROUPS, GROUP, WIDE), jnp.float32),
        compiler_params=params(32),
        cost_estimate=pl.CostEstimate(flops=400 << 20, bytes_accessed=4 << 20, transcendentals=0),
    )(norm, raw_traces, rim, weights, jnp.repeat(station_shifts, 3)[:, None])
    traces = lax.all_to_all(traces, ("y", "xl"), 0, 0, tiled=True)

    powers = jnp.sum(traces[:, :, WIDE - 1], axis=0)
    norms = traces[:, USED, 0]
    facts = jnp.concatenate([powers, norms, jnp.zeros((LANES - GROUP - GROUPS,), jnp.float32)])
    along = lax.axis_size(("zq", "zp"))
    facts = jnp.broadcast_to(facts[None], (along, LANES))
    facts = lax.all_to_all(facts, ("zq", "zp"), 0, 0, tiled=True)
    powers = jnp.sum(facts[:, :GROUP], axis=0)
    root_power = jnp.sqrt(powers / (lags * blocks) + 1e-06)
    norms = facts[:, GROUP : GROUP + GROUPS].T.reshape(4, 1, 2 * along)
    norms = jnp.sum(lax.all_to_all(norms, ("xh", "core"), 0, 0, tiled=True), axis=(0, 1))
    root_power, norms = lax.optimization_barrier((root_power, norms))

    sums = correlate(gathered, traces, root_power[:, None], lags)
    sums = sums.reshape(4 * GROUPS, 32, lags)
    sums = lax.all_to_all(sums, ("core", "xh", "y", "xl"), 0, 0, tiled=True)
    sums = jnp.sum(sums.astype(jnp.float32), axis=0)
    return sums / jnp.sqrt(norms + 1e-05)[:, None]


def solution(mesh):
    fine = Mesh(
        mesh.devices.reshape(2, 4, 2, 8, 2, 2), ("xh", "y", "xl", "zq", "zp", "core")
    )
    parts = ("xh", "core")
    return jax.shard_map(
        local,
        mesh=fine,
        in_specs=(P(parts, BLK), P(), P(BLK, parts, None), P(BLK), P(BLK, parts), P(parts)),
        out_specs=P(parts, BLK),
        check_vma=False,
    )
```

```python
import jax
import jax.numpy as jnp
import numpy as np
from jax import lax
from jax.experimental import pallas as pl
from jax.experimental.pallas import tpu as pltpu
from jax.sharding import Mesh, PartitionSpec as P

TLEN = 128
NTAP = 60
DECIM = 5
SHIFT_MAX = 64
LANES = 128
SUB = 16
ROWS = TLEN // SUB
PAIR = 2
WIDE = 640
GROUPS = 8
GROUP = 40
USED = 38
RIM = 192
PIECES = 4
BLK = ("y", "xl", "zq", "zp")


def vmem():
    return pl.BlockSpec(memory_space=pltpu.VMEM)


def params(mib):
    return pltpu.CompilerParams(vmem_limit_bytes=mib << 20)


def from_next_block(value):
    count = 128
    return lax.ppermute(value, BLK, [(i + 1, i) for i in range(count - 1)])


def product(left, right):
    dims = (((1,), (1,)), ((), ()))
    return lax.dot_general(left, right, dims, preferred_element_type=jnp.float32)


def front_kernel(
    start_ref, taps_ref, template_ref, mask_ref, order_ref, raw_ref,
    message_ref, rim_ref, norm_ref, weights_ref,
):
    step = DECIM * LANES
    taps = jnp.broadcast_to(taps_ref[...].astype(jnp.float32), (8, LANES))
    taps = pltpu.roll(taps, 0, 1, stride=DECIM, stride_axis=0)
    taps = jnp.concatenate([taps, jnp.zeros((8, step), jnp.float32)], axis=1)
    tiles = [taps] + [pltpu.roll(taps, 8 * DECIM * i, 1) for i in range(1, LANES // 8)]
    weights_ref[...] = jnp.concatenate(tiles, axis=0).astype(jnp.bfloat16)
    rim_ref[:, :LANES] = product(raw_ref[:, : step + LANES], weights_ref[...])
    later = product(raw_ref[:, step : 2 * step + LANES], weights_ref[...])
    raw = pltpu.roll(raw_ref[:, :LANES].astype(jnp.float32), RIM % LANES, 1)
    lane = lax.broadcasted_iota(jnp.int32, raw.shape, 1)
    rim_ref[:, LANES:] = jnp.where(lane < RIM % LANES, later, raw)

    stored = template_ref[0].astype(jnp.float32)
    channels, width = stored.shape
    window = pltpu.roll(stored, lax.rem(width - start_ref[0], width), 1)[:, :TLEN]
    spare = -channels % LANES
    window = jnp.concatenate([window, jnp.zeros((spare, TLEN), jnp.float32)], axis=0)
    mask = mask_ref[...].astype(jnp.float32)
    mask = jnp.concatenate([mask, jnp.zeros((1, spare), jnp.float32)], axis=1)
    panel = window.T * mask
    norm = jnp.sum(jnp.sum(panel * panel, axis=0, keepdims=True), axis=1, keepdims=True)
    norm_ref[...] = jnp.broadcast_to(norm, norm_ref.shape)

    mixed = jnp.dot(
        order_ref[...], panel.astype(jnp.bfloat16), preferred_element_type=jnp.float32
    )
    lane = lax.broadcasted_iota(jnp.int32, (ROWS, WIDE), 1)
    empty = jnp.zeros((ROWS, WIDE), jnp.float32)
    messages = [empty] * GROUPS
    for s in range(SUB):
        row = mixed[s * ROWS : (s + 1) * ROWS]
        row = jnp.concatenate([row, empty[:, row.shape[1] :]], axis=1)
        place = (lane >= s * GROUP) & (lane < s * GROUP + USED)
        for g in range(GROUPS):
            hop = (s * GROUP - g * USED) % WIDE
            moved = row if hop == 0 else pltpu.roll(row, hop, 1)
            messages[g] = jnp.where(place, moved, messages[g])
    for g in range(GROUPS):
        message = messages[g].astype(jnp.bfloat16)
        message_ref[2 * g] = message
        message_ref[2 * g + 1] = message


def trace_kernel(norm_ref, raw_ref, rim_ref, weights_ref, shift_ref, out_ref):
    channels = raw_ref.shape[0]
    step = DECIM * LANES
    own = raw_ref.shape[1] // step
    blocks = []
    for i in range(own - 1):
        blocks.append(product(raw_ref[:, i * step : i * step + step + LANES], weights_ref[...]))
    raw_rim = pltpu.roll(rim_ref[:, LANES:], LANES - RIM % LANES, 1).astype(jnp.bfloat16)
    blocks.append(
        product(raw_ref[:, (own - 1) * step :], weights_ref[:, :step])
        + product(raw_rim, weights_ref[:, step:])
    )
    blocks.append(rim_ref[...])
    squares = blocks[0] * blocks[0]
    for block in blocks[1:own]:
        squares = squares + block * block
    power = jnp.sum(squares, axis=1, keepdims=True)

    rows = jnp.concatenate(blocks, axis=1)
    shift = shift_ref[...]
    width = rows.shape[1]
    for bit in range(SHIFT_MAX.bit_length()):
        hop = 1 << bit
        moved = pltpu.roll(rows, width - hop, 1)
        rows = jnp.where((shift & hop) != 0, moved, rows)
    rows = rows[:, :WIDE]
    lane = lax.broadcasted_iota(jnp.int32, rows.shape, 1)
    rows = jnp.where(lane == WIDE - 1, power, rows)
    spare = GROUP - USED
    side = lax.broadcasted_iota(jnp.int32, (spare, WIDE), 0)
    side = jnp.where(side == 0, jnp.broadcast_to(norm_ref[:, :1], side.shape), 0.0)
    for g in range(GROUPS):
        first, last = g * USED, min((g + 1) * USED, channels)
        pieces = [rows[first:last]]
        if last - first < USED:
            pieces.append(jnp.zeros((USED - last + first, WIDE), jnp.float32))
        out_ref[g] = jnp.concatenate(pieces + [side], axis=0)


def corr_kernel(
    panel_ref, first_ref, second_ref, trace_ref, root_ref, out_ref, mixed, panels, shifted
):
    chunks = panel_ref.shape[0] // LANES
    lags = out_ref.shape[-1]
    count = ROWS // PAIR

    @pl.when(pl.program_id(0) == 0)
    def _():
        for i in range(chunks):
            part = jnp.dot(
                first_ref[...], panel_ref[i * LANES : (i + 1) * LANES, :],
                preferred_element_type=jnp.float32,
            ).astype(jnp.bfloat16)
            for r in range(ROWS):
                mixed[r, i * SUB : (i + 1) * SUB, :] = part[r * SUB : (r + 1) * SUB, :]
        for r in range(ROWS):
            part = jnp.dot(
                second_ref[...], mixed[r], preferred_element_type=jnp.float32
            ).astype(jnp.bfloat16)
            a, h = divmod(r, PAIR)
            panels[a * LANES : (a + 1) * LANES, h * WIDE : (h + 1) * WIDE] = part

    pieces = trace_ref.shape[0]
    for t in range(pieces):
        trace = (trace_ref[t] / root_ref[...]).astype(jnp.bfloat16).astype(jnp.float32)
        for j in range(PAIR * SUB // 2):
            low = trace if j == 0 else pltpu.roll(trace, WIDE - 2 * j, 1)
            high = pltpu.roll(trace, WIDE - 2 * j - 1, 1)
            both = jnp.concatenate([low, high], axis=0).astype(jnp.bfloat16)
            shifted[j * 2 * GROUP : (j + 1) * 2 * GROUP, t * WIDE : (t + 1) * WIDE] = both
    sums = jnp.dot(panels[...], shifted[...], preferred_element_type=jnp.float32)
    for t in range(pieces):
        total = sums[:LANES, t * WIDE : t * WIDE + lags]
        for a in range(1, count):
            part = sums[a * LANES : (a + 1) * LANES, t * WIDE : (t + 1) * WIDE]
            total = total + pltpu.roll(part, WIDE - a * PAIR * SUB, 1)[:, :lags]
        for c in range(2):
            for x in range(2):
                g = c * 2 + x
                out_ref[c, x, t] = total[g * 32 : (g + 1) * 32, :]


def orders():
    first = np.zeros((LANES, LANES), np.float32)
    for src in range(SUB):
        for r in range(ROWS):
            first[r * SUB + src, src * ROWS + r] = 1
    second = np.zeros((LANES, LANES), np.float32)
    for zq in range(8):
        for y in range(4):
            for xl in range(2):
                for zp in range(2):
                    source = ((zq * 4 + y) * 2 + xl) * 2 + zp
                    x, c = divmod(y, 2)
                    target = (((c * 2 + x) * 2 + xl) * 8 + zq) * 2 + zp
                    second[target, source] = 1
    return jnp.asarray(first, jnp.bfloat16), jnp.asarray(second, jnp.bfloat16)


def whole(shape):
    return pl.BlockSpec(shape, lambda i: (0,) * len(shape))


def correlate(gathered, traces, root_power, lags):
    first, second = orders()
    depth = PAIR * SUB * GROUP
    flops = 2 * ROWS // PAIR * LANES * depth * WIDE * GROUPS
    return pl.pallas_call(
        corr_kernel,
        grid=(GROUPS // PIECES,),
        in_specs=[
            whole(gathered.shape),
            whole(first.shape),
            whole(second.shape),
            pl.BlockSpec((PIECES, GROUP, WIDE), lambda i: (i, 0, 0)),
            whole(root_power.shape),
        ],
        out_specs=pl.BlockSpec((2, 2, PIECES, 32, lags), lambda i: (0, 0, i, 0, 0)),
        out_shape=jax.ShapeDtypeStruct((2, 2, GROUPS, 32, lags), jnp.float32),
        scratch_shapes=[
            pltpu.VMEM((ROWS, LANES, WIDE), jnp.bfloat16),
            pltpu.VMEM((ROWS // PAIR * LANES, depth), jnp.bfloat16),
            pltpu.VMEM((depth, PIECES * WIDE), jnp.bfloat16),
        ],
        compiler_params=params(48),
        cost_estimate=pl.CostEstimate(flops=flops, bytes_accessed=4 << 20, transcendentals=0),
    )(gathered, first, second, traces, root_power)


def local(raw_traces, fir_taps, templates, start_offsets, channel_mask, station_shifts):
    channels, raw_len = raw_traces.shape
    lags = raw_len // DECIM
    blocks = lax.axis_size(BLK)
    order = np.zeros((TLEN, TLEN), np.float32)
    for r in range(ROWS):
        for s in range(SUB):
            order[s * ROWS + r, r * SUB + s] = 1
    depth = DECIM * LANES + LANES
    taps = jnp.pad(fir_taps, (0, LANES - NTAP))[None]
    near = (channels, 2 * DECIM * LANES + LANES)
    message, rim, norm, weights = pl.pallas_call(
        front_kernel,
        grid=(1,),
        in_specs=[
            pl.BlockSpec(memory_space=pltpu.SMEM),
            whole(taps.shape),
            whole(templates.shape),
            whole(channel_mask.shape),
            whole(order.shape),
            whole(near),
        ],
        out_specs=[
            whole((2 * GROUPS, ROWS, WIDE)),
            whole((channels, 2 * LANES)),
            whole((1, LANES)),
            whole((LANES, depth)),
        ],
        out_shape=[
            jax.ShapeDtypeStruct((2 * GROUPS, ROWS, WIDE), jnp.bfloat16),
            jax.ShapeDtypeStruct((channels, 2 * LANES), jnp.float32),
            jax.ShapeDtypeStruct((1, LANES), jnp.float32),
            jax.ShapeDtypeStruct((LANES, depth), jnp.bfloat16),
        ],
        compiler_params=params(63),
        cost_estimate=pl.CostEstimate(flops=128 << 20, bytes_accessed=2 << 20, transcendentals=0),
    )(start_offsets, taps, templates, channel_mask, jnp.asarray(order, jnp.bfloat16), raw_traces)
    rim = from_next_block(rim)
    exchanged = lax.all_to_all(message, ("y", "xl", "zp"), 0, 0, tiled=True)
    exchanged, rim = lax.optimization_barrier((exchanged, rim))
    gathered = lax.all_gather(exchanged, "zq", axis=0, tiled=True)
    gathered = gathered.reshape(blocks * ROWS, SUB * GROUP)

    traces = pl.pallas_call(
        trace_kernel,
        in_specs=[vmem()] * 5,
        out_specs=vmem(),
        out_shape=jax.ShapeDtypeStruct((GROUPS, GROUP, WIDE), jnp.float32),
        compiler_params=params(32),
        cost_estimate=pl.CostEstimate(flops=400 << 20, bytes_accessed=4 << 20, transcendentals=0),
    )(norm, raw_traces, rim, weights, jnp.repeat(station_shifts, 3)[:, None])
    traces = lax.all_to_all(traces, ("y", "xl"), 0, 0, tiled=True)

    powers = jnp.sum(traces[:, :, WIDE - 1], axis=0)
    norms = traces[:, USED, 0]
    facts = jnp.concatenate([powers, norms, jnp.zeros((LANES - GROUP - GROUPS,), jnp.float32)])
    along = lax.axis_size(("zq", "zp"))
    facts = jnp.broadcast_to(facts[None], (along, LANES))
    facts = lax.all_to_all(facts, ("zq", "zp"), 0, 0, tiled=True)
    powers = jnp.sum(facts[:, :GROUP], axis=0)
    root_power = jnp.sqrt(powers / (lags * blocks) + 1e-06)
    norms = facts[:, GROUP : GROUP + GROUPS].T.reshape(4, 1, 2 * along)
    norms = jnp.sum(lax.all_to_all(norms, ("xh", "core"), 0, 0, tiled=True), axis=(0, 1))
    root_power, norms = lax.optimization_barrier((root_power, norms))

    sums = correlate(gathered, traces, root_power[:, None], lags)
    sums = jnp.sum(lax.all_to_all(sums, "core", 0, 0, tiled=True), axis=0)
    sums = sums.astype(jnp.bfloat16).reshape(2 * GROUPS, 32, lags)
    sums = lax.all_to_all(sums, ("xh", "y", "xl"), 0, 0, tiled=True)
    sums = jnp.sum(sums.astype(jnp.float32), axis=0)
    return sums / jnp.sqrt(norms + 1e-05)[:, None]


def solution(mesh):
    fine = Mesh(
        mesh.devices.reshape(2, 4, 2, 8, 2, 2), ("xh", "y", "xl", "zq", "zp", "core")
    )
    parts = ("xh", "core")
    return jax.shard_map(
        local,
        mesh=fine,
        in_specs=(P(parts, BLK), P(), P(BLK, parts, None), P(BLK), P(BLK, parts), P(parts)),
        out_specs=P(parts, BLK),
        check_vma=False,
    )
```

```python
import jax
import jax.numpy as jnp
import numpy as np
from jax import lax
from jax.experimental import pallas as pl
from jax.experimental.pallas import tpu as pltpu
from jax.sharding import Mesh, PartitionSpec as P

TLEN = 128
NTAP = 60
DECIM = 5
SHIFT_MAX = 64
LANES = 128
SUB = 16
ROWS = TLEN // SUB
PAIR = 2
WIDE = 640
GROUPS = 8
GROUP = 40
USED = 38
RIM = 192
PIECES = 4
BLK = ("y", "xl", "zq", "zp")


def vmem():
    return pl.BlockSpec(memory_space=pltpu.VMEM)


def params(mib):
    return pltpu.CompilerParams(vmem_limit_bytes=mib << 20)


def from_next_block(value):
    count = 128
    return lax.ppermute(value, BLK, [(i + 1, i) for i in range(count - 1)])


def product(left, right):
    dims = (((1,), (1,)), ((), ()))
    return lax.dot_general(left, right, dims, preferred_element_type=jnp.float32)


def front_kernel(
    start_ref, taps_ref, template_ref, mask_ref, order_ref, raw_ref,
    message_ref, rim_ref, norm_ref, weights_ref,
):
    step = DECIM * LANES
    taps = jnp.broadcast_to(taps_ref[...].astype(jnp.float32), (8, NTAP))
    taps = jnp.concatenate([taps, jnp.zeros((8, LANES - NTAP), jnp.float32)], axis=1)
    taps = pltpu.roll(taps, 0, 1, stride=DECIM, stride_axis=0)
    taps = jnp.concatenate([taps, jnp.zeros((8, step), jnp.float32)], axis=1)
    tiles = [taps] + [pltpu.roll(taps, 8 * DECIM * i, 1) for i in range(1, LANES // 8)]
    weights_ref[...] = jnp.concatenate(tiles, axis=0).astype(jnp.bfloat16)
    rim_ref[:, :LANES] = product(raw_ref[:, : step + LANES], weights_ref[...])
    later = product(raw_ref[:, step : 2 * step + LANES], weights_ref[...])
    raw = pltpu.roll(raw_ref[:, :LANES].astype(jnp.float32), RIM % LANES, 1)
    lane = lax.broadcasted_iota(jnp.int32, raw.shape, 1)
    rim_ref[:, LANES:] = jnp.where(lane < RIM % LANES, later, raw)

    stored = template_ref[0].astype(jnp.float32)
    channels, width = stored.shape
    window = pltpu.roll(stored, lax.rem(width - start_ref[0], width), 1)[:, :TLEN]
    spare = -channels % LANES
    window = jnp.concatenate([window, jnp.zeros((spare, TLEN), jnp.float32)], axis=0)
    mask = mask_ref[...].astype(jnp.float32)
    mask = jnp.concatenate([mask, jnp.zeros((1, spare), jnp.float32)], axis=1)
    panel = window.T * mask
    norm = jnp.sum(jnp.sum(panel * panel, axis=0, keepdims=True), axis=1, keepdims=True)
    norm_ref[...] = jnp.broadcast_to(norm, norm_ref.shape)

    mixed = jnp.dot(
        order_ref[...], panel.astype(jnp.bfloat16), preferred_element_type=jnp.float32
    )
    lane = lax.broadcasted_iota(jnp.int32, (ROWS, WIDE), 1)
    empty = jnp.zeros((ROWS, WIDE), jnp.float32)
    messages = [empty] * GROUPS
    for s in range(SUB):
        row = mixed[s * ROWS : (s + 1) * ROWS]
        row = jnp.concatenate([row, empty[:, row.shape[1] :]], axis=1)
        place = (lane >= s * GROUP) & (lane < s * GROUP + USED)
        for g in range(GROUPS):
            hop = (s * GROUP - g * USED) % WIDE
            moved = row if hop == 0 else pltpu.roll(row, hop, 1)
            messages[g] = jnp.where(place, moved, messages[g])
    for g in range(GROUPS):
        message = messages[g].astype(jnp.bfloat16)
        message_ref[2 * g] = message
        message_ref[2 * g + 1] = message


def trace_kernel(norm_ref, raw_ref, rim_ref, weights_ref, shift_ref, out_ref):
    channels = raw_ref.shape[0]
    step = DECIM * LANES
    own = raw_ref.shape[1] // step
    blocks = []
    for i in range(own - 1):
        blocks.append(product(raw_ref[:, i * step : i * step + step + LANES], weights_ref[...]))
    raw_rim = pltpu.roll(rim_ref[:, LANES:], LANES - RIM % LANES, 1).astype(jnp.bfloat16)
    blocks.append(
        product(raw_ref[:, (own - 1) * step :], weights_ref[:, :step])
        + product(raw_rim, weights_ref[:, step:])
    )
    blocks.append(rim_ref[...])
    squares = blocks[0] * blocks[0]
    for block in blocks[1:own]:
        squares = squares + block * block
    power = jnp.sum(squares, axis=1, keepdims=True)

    rows = jnp.concatenate(blocks, axis=1)
    shift = shift_ref[...]
    width = rows.shape[1]
    for bit in range(SHIFT_MAX.bit_length()):
        hop = 1 << bit
        moved = pltpu.roll(rows, width - hop, 1)
        rows = jnp.where((shift & hop) != 0, moved, rows)
    rows = rows[:, :WIDE]
    lane = lax.broadcasted_iota(jnp.int32, rows.shape, 1)
    rows = jnp.where(lane == WIDE - 1, power, rows)
    spare = GROUP - USED
    side = lax.broadcasted_iota(jnp.int32, (spare, WIDE), 0)
    side = jnp.where(side == 0, jnp.broadcast_to(norm_ref[:, :1], side.shape), 0.0)
    for g in range(GROUPS):
        first, last = g * USED, min((g + 1) * USED, channels)
        pieces = [rows[first:last]]
        if last - first < USED:
            pieces.append(jnp.zeros((USED - last + first, WIDE), jnp.float32))
        out_ref[g] = jnp.concatenate(pieces + [side], axis=0)


def corr_kernel(
    panel_ref, first_ref, second_ref, trace_ref, root_ref, out_ref, mixed, panels, shifted
):
    chunks = panel_ref.shape[0] // LANES
    lags = out_ref.shape[-1]
    count = ROWS // PAIR

    @pl.when(pl.program_id(0) == 0)
    def _():
        for i in range(chunks):
            part = jnp.dot(
                first_ref[...], panel_ref[i * LANES : (i + 1) * LANES, :],
                preferred_element_type=jnp.float32,
            ).astype(jnp.bfloat16)
            for r in range(ROWS):
                mixed[r, i * SUB : (i + 1) * SUB, :] = part[r * SUB : (r + 1) * SUB, :]
        for r in range(ROWS):
            part = jnp.dot(
                second_ref[...], mixed[r], preferred_element_type=jnp.float32
            ).astype(jnp.bfloat16)
            a, h = divmod(r, PAIR)
            panels[a * LANES : (a + 1) * LANES, h * WIDE : (h + 1) * WIDE] = part

    pieces = trace_ref.shape[0]
    for t in range(pieces):
        trace = (trace_ref[t] / root_ref[...]).astype(jnp.bfloat16).astype(jnp.float32)
        for j in range(PAIR * SUB // 2):
            low = trace if j == 0 else pltpu.roll(trace, WIDE - 2 * j, 1)
            high = pltpu.roll(trace, WIDE - 2 * j - 1, 1)
            both = jnp.concatenate([low, high], axis=0).astype(jnp.bfloat16)
            shifted[j * 2 * GROUP : (j + 1) * 2 * GROUP, t * WIDE : (t + 1) * WIDE] = both
    sums = jnp.dot(panels[...], shifted[...], preferred_element_type=jnp.float32)
    for t in range(pieces):
        total = sums[:LANES, t * WIDE : t * WIDE + lags]
        for a in range(1, count):
            part = sums[a * LANES : (a + 1) * LANES, t * WIDE : (t + 1) * WIDE]
            total = total + pltpu.roll(part, WIDE - a * PAIR * SUB, 1)[:, :lags]
        for c in range(2):
            for x in range(2):
                g = c * 2 + x
                out_ref[c, x, t] = total[g * 32 : (g + 1) * 32, :]


def orders():
    first = np.zeros((LANES, LANES), np.float32)
    for src in range(SUB):
        for r in range(ROWS):
            first[r * SUB + src, src * ROWS + r] = 1
    second = np.zeros((LANES, LANES), np.float32)
    for zq in range(8):
        for y in range(4):
            for xl in range(2):
                for zp in range(2):
                    source = ((zq * 4 + y) * 2 + xl) * 2 + zp
                    x, c = divmod(y, 2)
                    target = (((c * 2 + x) * 2 + xl) * 8 + zq) * 2 + zp
                    second[target, source] = 1
    return jnp.asarray(first, jnp.bfloat16), jnp.asarray(second, jnp.bfloat16)


def whole(shape):
    return pl.BlockSpec(shape, lambda i: (0,) * len(shape))


def correlate(gathered, traces, root_power, lags):
    first, second = orders()
    depth = PAIR * SUB * GROUP
    flops = 2 * ROWS // PAIR * LANES * depth * WIDE * GROUPS
    return pl.pallas_call(
        corr_kernel,
        grid=(GROUPS // PIECES,),
        in_specs=[
            whole(gathered.shape),
            whole(first.shape),
            whole(second.shape),
            pl.BlockSpec((PIECES, GROUP, WIDE), lambda i: (i, 0, 0)),
            whole(root_power.shape),
        ],
        out_specs=pl.BlockSpec((2, 2, PIECES, 32, lags), lambda i: (0, 0, i, 0, 0)),
        out_shape=jax.ShapeDtypeStruct((2, 2, GROUPS, 32, lags), jnp.float32),
        scratch_shapes=[
            pltpu.VMEM((ROWS, LANES, WIDE), jnp.bfloat16),
            pltpu.VMEM((ROWS // PAIR * LANES, depth), jnp.bfloat16),
            pltpu.VMEM((depth, PIECES * WIDE), jnp.bfloat16),
        ],
        compiler_params=params(48),
        cost_estimate=pl.CostEstimate(flops=flops, bytes_accessed=4 << 20, transcendentals=0),
    )(gathered, first, second, traces, root_power)


def local(raw_traces, fir_taps, templates, start_offsets, channel_mask, station_shifts):
    channels, raw_len = raw_traces.shape
    lags = raw_len // DECIM
    blocks = lax.axis_size(BLK)
    order = np.zeros((TLEN, TLEN), np.float32)
    for r in range(ROWS):
        for s in range(SUB):
            order[s * ROWS + r, r * SUB + s] = 1
    depth = DECIM * LANES + LANES
    taps = fir_taps[None]
    near = (channels, 2 * DECIM * LANES + LANES)
    message, rim, norm, weights = pl.pallas_call(
        front_kernel,
        grid=(1,),
        in_specs=[
            pl.BlockSpec(memory_space=pltpu.SMEM),
            whole(taps.shape),
            whole(templates.shape),
            whole(channel_mask.shape),
            whole(order.shape),
            whole(near),
        ],
        out_specs=[
            whole((2 * GROUPS, ROWS, WIDE)),
            whole((channels, 2 * LANES)),
            whole((1, LANES)),
            whole((LANES, depth)),
        ],
        out_shape=[
            jax.ShapeDtypeStruct((2 * GROUPS, ROWS, WIDE), jnp.bfloat16),
            jax.ShapeDtypeStruct((channels, 2 * LANES), jnp.float32),
            jax.ShapeDtypeStruct((1, LANES), jnp.float32),
            jax.ShapeDtypeStruct((LANES, depth), jnp.bfloat16),
        ],
        compiler_params=params(63),
        cost_estimate=pl.CostEstimate(flops=128 << 20, bytes_accessed=2 << 20, transcendentals=0),
    )(start_offsets, taps, templates, channel_mask, jnp.asarray(order, jnp.bfloat16), raw_traces)
    rim = from_next_block(rim)
    exchanged = lax.all_to_all(message, ("y", "xl", "zp"), 0, 0, tiled=True)
    exchanged, rim = lax.optimization_barrier((exchanged, rim))
    gathered = lax.all_gather(exchanged, "zq", axis=0, tiled=True)
    gathered = gathered.reshape(blocks * ROWS, SUB * GROUP)

    traces = pl.pallas_call(
        trace_kernel,
        in_specs=[vmem()] * 5,
        out_specs=vmem(),
        out_shape=jax.ShapeDtypeStruct((GROUPS, GROUP, WIDE), jnp.float32),
        compiler_params=params(32),
        cost_estimate=pl.CostEstimate(flops=400 << 20, bytes_accessed=4 << 20, transcendentals=0),
    )(norm, raw_traces, rim, weights, jnp.repeat(station_shifts, 3)[:, None])
    traces = lax.all_to_all(traces, ("y", "xl"), 0, 0, tiled=True)

    powers = jnp.sum(traces[:, :, WIDE - 1], axis=0)
    norms = traces[:, USED, 0]
    facts = jnp.concatenate([powers, norms, jnp.zeros((LANES - GROUP - GROUPS,), jnp.float32)])
    along = lax.axis_size(("zq", "zp"))
    facts = jnp.broadcast_to(facts[None], (along, LANES))
    facts = lax.all_to_all(facts, ("zq", "zp"), 0, 0, tiled=True)
    powers = jnp.sum(facts[:, :GROUP], axis=0)
    root_power = jnp.sqrt(powers / (lags * blocks) + 1e-06)
    norms = facts[:, GROUP : GROUP + GROUPS].T.reshape(4, 1, 2 * along)
    norms = jnp.sum(lax.all_to_all(norms, ("xh", "core"), 0, 0, tiled=True), axis=(0, 1))
    root_power, norms = lax.optimization_barrier((root_power, norms))

    sums = correlate(gathered, traces, root_power[:, None], lags)
    sums = jnp.sum(lax.all_to_all(sums, "core", 0, 0, tiled=True), axis=0)
    sums = sums.astype(jnp.bfloat16).reshape(2 * GROUPS, 32, lags)
    sums = lax.all_to_all(sums, ("xh", "y", "xl"), 0, 0, tiled=True)
    sums = jnp.sum(sums.astype(jnp.float32), axis=0)
    return sums / jnp.sqrt(norms + 1e-05)[:, None]


def solution(mesh):
    fine = Mesh(
        mesh.devices.reshape(2, 4, 2, 8, 2, 2), ("xh", "y", "xl", "zq", "zp", "core")
    )
    parts = ("xh", "core")
    return jax.shard_map(
        local,
        mesh=fine,
        in_specs=(P(parts, BLK), P(), P(BLK, parts, None), P(BLK), P(BLK, parts), P(parts)),
        out_specs=P(parts, BLK),
        check_vma=False,
    )
```

```python
import jax
import jax.numpy as jnp
import numpy as np
from jax import lax
from jax.experimental import pallas as pl
from jax.experimental.pallas import tpu as pltpu
from jax.sharding import Mesh, PartitionSpec as P

TLEN = 128
NTAP = 60
DECIM = 5
SHIFT_MAX = 64
LANES = 128
SUB = 16
ROWS = TLEN // SUB
PAIR = 2
WIDE = 640
GROUPS = 8
GROUP = 40
USED = 38
RIM = 192
PIECES = 4
BLK = ("y", "xl", "zq", "zp")


def vmem():
    return pl.BlockSpec(memory_space=pltpu.VMEM)


def params(mib):
    return pltpu.CompilerParams(vmem_limit_bytes=mib << 20)


def from_next_block(value):
    count = 128
    return lax.ppermute(value, BLK, [(i + 1, i) for i in range(count - 1)])


def product(left, right):
    dims = (((1,), (1,)), ((), ()))
    return lax.dot_general(left, right, dims, preferred_element_type=jnp.float32)


def front_kernel(
    start_ref, taps_ref, template_ref, mask_ref, order_ref, raw_ref,
    message_ref, rim_ref, norm_ref, weights_ref,
):
    step = DECIM * LANES
    taps = jnp.broadcast_to(taps_ref[...].astype(jnp.float32), (8, NTAP))
    taps = jnp.concatenate([taps, jnp.zeros((8, LANES - NTAP), jnp.float32)], axis=1)
    taps = pltpu.roll(taps, 0, 1, stride=DECIM, stride_axis=0)
    taps = jnp.concatenate([taps, jnp.zeros((8, step), jnp.float32)], axis=1)
    tiles = [taps] + [pltpu.roll(taps, 8 * DECIM * i, 1) for i in range(1, LANES // 8)]
    weights_ref[...] = jnp.concatenate(tiles, axis=0).astype(jnp.bfloat16)
    rim_ref[:, :LANES] = product(raw_ref[:, : step + LANES], weights_ref[...])
    later = product(raw_ref[:, step : 2 * step + LANES], weights_ref[...])
    raw = pltpu.roll(raw_ref[:, :LANES].astype(jnp.float32), RIM % LANES, 1)
    lane = lax.broadcasted_iota(jnp.int32, raw.shape, 1)
    rim_ref[:, LANES:] = jnp.where(lane < RIM % LANES, later, raw)

    stored = template_ref[0].astype(jnp.float32)
    channels, width = stored.shape
    window = pltpu.roll(stored, lax.rem(width - start_ref[0], width), 1)[:, :TLEN]
    spare = -channels % LANES
    window = jnp.concatenate([window, jnp.zeros((spare, TLEN), jnp.float32)], axis=0)
    mask = mask_ref[...].astype(jnp.float32)
    mask = jnp.concatenate([mask, jnp.zeros((1, spare), jnp.float32)], axis=1)
    panel = window.T * mask
    norm = jnp.sum(jnp.sum(panel * panel, axis=0, keepdims=True), axis=1, keepdims=True)
    norm_ref[...] = jnp.broadcast_to(norm, norm_ref.shape)

    mixed = jnp.dot(
        order_ref[...], panel.astype(jnp.bfloat16), preferred_element_type=jnp.float32
    )
    lane = lax.broadcasted_iota(jnp.int32, (ROWS, WIDE), 1)
    empty = jnp.zeros((ROWS, WIDE), jnp.float32)
    messages = [empty] * GROUPS
    for s in range(SUB):
        row = mixed[s * ROWS : (s + 1) * ROWS]
        row = jnp.concatenate([row, empty[:, row.shape[1] :]], axis=1)
        place = (lane >= s * GROUP) & (lane < s * GROUP + USED)
        for g in range(GROUPS):
            hop = (s * GROUP - g * USED) % WIDE
            moved = row if hop == 0 else pltpu.roll(row, hop, 1)
            messages[g] = jnp.where(place, moved, messages[g])
    for g in range(GROUPS):
        message = messages[g].astype(jnp.bfloat16)
        message_ref[2 * g] = message
        message_ref[2 * g + 1] = message


def trace_kernel(norm_ref, raw_ref, rim_ref, weights_ref, shift_ref, out_ref):
    channels = raw_ref.shape[0]
    step = DECIM * LANES
    own = raw_ref.shape[1] // step
    blocks = []
    for i in range(own - 1):
        blocks.append(product(raw_ref[:, i * step : i * step + step + LANES], weights_ref[...]))
    raw_rim = pltpu.roll(rim_ref[:, LANES:], LANES - RIM % LANES, 1).astype(jnp.bfloat16)
    blocks.append(
        product(raw_ref[:, (own - 1) * step :], weights_ref[:, :step])
        + product(raw_rim, weights_ref[:, step:])
    )
    blocks.append(rim_ref[...])
    squares = blocks[0] * blocks[0]
    for block in blocks[1:own]:
        squares = squares + block * block
    power = jnp.sum(squares, axis=1, keepdims=True)

    rows = jnp.concatenate(blocks, axis=1)
    shift = shift_ref[...]
    width = rows.shape[1]
    for bit in range(SHIFT_MAX.bit_length()):
        hop = 1 << bit
        moved = pltpu.roll(rows, width - hop, 1)
        rows = jnp.where((shift & hop) != 0, moved, rows)
    rows = rows[:, :WIDE]
    lane = lax.broadcasted_iota(jnp.int32, rows.shape, 1)
    rows = jnp.where(lane == WIDE - 1, power, rows)
    spare = GROUP - USED
    side = lax.broadcasted_iota(jnp.int32, (spare, WIDE), 0)
    side = jnp.where(side == 0, jnp.broadcast_to(norm_ref[:, :1], side.shape), 0.0)
    for g in range(GROUPS):
        first, last = g * USED, min((g + 1) * USED, channels)
        pieces = [rows[first:last]]
        if last - first < USED:
            pieces.append(jnp.zeros((USED - last + first, WIDE), jnp.float32))
        out_ref[g] = jnp.concatenate(pieces + [side], axis=0)


def corr_kernel(
    panel_ref, first_ref, second_ref, trace_ref, root_ref, out_ref, mixed, panels, shifted
):
    chunks = panel_ref.shape[0] // LANES
    lags = out_ref.shape[-1]
    count = ROWS // PAIR

    @pl.when(pl.program_id(0) == 0)
    def _():
        for i in range(chunks):
            part = jnp.dot(
                first_ref[...], panel_ref[i * LANES : (i + 1) * LANES, :],
                preferred_element_type=jnp.float32,
            ).astype(jnp.bfloat16)
            for r in range(ROWS):
                mixed[r, i * SUB : (i + 1) * SUB, :] = part[r * SUB : (r + 1) * SUB, :]
        for r in range(ROWS):
            part = jnp.dot(
                second_ref[...], mixed[r], preferred_element_type=jnp.float32
            ).astype(jnp.bfloat16)
            a, h = divmod(r, PAIR)
            panels[a * LANES : (a + 1) * LANES, h * WIDE : (h + 1) * WIDE] = part

    pieces = trace_ref.shape[0]
    for t in range(pieces):
        trace = (trace_ref[t] / root_ref[...]).astype(jnp.bfloat16).astype(jnp.float32)
        for j in range(PAIR * SUB // 2):
            low = trace if j == 0 else pltpu.roll(trace, WIDE - 2 * j, 1)
            high = pltpu.roll(trace, WIDE - 2 * j - 1, 1)
            both = jnp.concatenate([low, high], axis=0).astype(jnp.bfloat16)
            shifted[j * 2 * GROUP : (j + 1) * 2 * GROUP, t * WIDE : (t + 1) * WIDE] = both
    sums = jnp.dot(panels[...], shifted[...], preferred_element_type=jnp.float32)
    for t in range(pieces):
        total = sums[:LANES, t * WIDE : t * WIDE + lags]
        for a in range(1, count):
            part = sums[a * LANES : (a + 1) * LANES, t * WIDE : (t + 1) * WIDE]
            total = total + pltpu.roll(part, WIDE - a * PAIR * SUB, 1)[:, :lags]
        for c in range(2):
            for x in range(2):
                g = c * 2 + x
                out_ref[c, x, t] = total[g * 32 : (g + 1) * 32, :]


def orders():
    first = np.zeros((LANES, LANES), np.float32)
    for src in range(SUB):
        for r in range(ROWS):
            first[r * SUB + src, src * ROWS + r] = 1
    second = np.zeros((LANES, LANES), np.float32)
    for zq in range(8):
        for y in range(4):
            for xl in range(2):
                for zp in range(2):
                    source = ((zq * 4 + y) * 2 + xl) * 2 + zp
                    x, c = divmod(y, 2)
                    target = (((c * 2 + x) * 2 + xl) * 8 + zq) * 2 + zp
                    second[target, source] = 1
    return jnp.asarray(first, jnp.bfloat16), jnp.asarray(second, jnp.bfloat16)


def whole(shape):
    return pl.BlockSpec(shape, lambda i: (0,) * len(shape))


def correlate(gathered, traces, root_power, lags):
    first, second = orders()
    depth = PAIR * SUB * GROUP
    flops = 2 * ROWS // PAIR * LANES * depth * WIDE * GROUPS
    return pl.pallas_call(
        corr_kernel,
        grid=(GROUPS // PIECES,),
        in_specs=[
            whole(gathered.shape),
            whole(first.shape),
            whole(second.shape),
            pl.BlockSpec((PIECES, GROUP, WIDE), lambda i: (i, 0, 0)),
            whole(root_power.shape),
        ],
        out_specs=pl.BlockSpec((2, 2, PIECES, 32, lags), lambda i: (0, 0, i, 0, 0)),
        out_shape=jax.ShapeDtypeStruct((2, 2, GROUPS, 32, lags), jnp.float32),
        scratch_shapes=[
            pltpu.VMEM((ROWS, LANES, WIDE), jnp.bfloat16),
            pltpu.VMEM((ROWS // PAIR * LANES, depth), jnp.bfloat16),
            pltpu.VMEM((depth, PIECES * WIDE), jnp.bfloat16),
        ],
        compiler_params=params(63),
        cost_estimate=pl.CostEstimate(flops=flops, bytes_accessed=4 << 20, transcendentals=0),
    )(gathered, first, second, traces, root_power)


def local(raw_traces, fir_taps, templates, start_offsets, channel_mask, station_shifts):
    channels, raw_len = raw_traces.shape
    lags = raw_len // DECIM
    blocks = lax.axis_size(BLK)
    order = np.zeros((TLEN, TLEN), np.float32)
    for r in range(ROWS):
        for s in range(SUB):
            order[s * ROWS + r, r * SUB + s] = 1
    depth = DECIM * LANES + LANES
    taps = fir_taps[None]
    near = (channels, 2 * DECIM * LANES + LANES)
    message, rim, norm, weights = pl.pallas_call(
        front_kernel,
        grid=(1,),
        in_specs=[
            pl.BlockSpec(memory_space=pltpu.SMEM),
            whole(taps.shape),
            whole(templates.shape),
            whole(channel_mask.shape),
            whole(order.shape),
            whole(near),
        ],
        out_specs=[
            whole((2 * GROUPS, ROWS, WIDE)),
            whole((channels, 2 * LANES)),
            whole((1, LANES)),
            whole((LANES, depth)),
        ],
        out_shape=[
            jax.ShapeDtypeStruct((2 * GROUPS, ROWS, WIDE), jnp.bfloat16),
            jax.ShapeDtypeStruct((channels, 2 * LANES), jnp.float32),
            jax.ShapeDtypeStruct((1, LANES), jnp.float32),
            jax.ShapeDtypeStruct((LANES, depth), jnp.bfloat16),
        ],
        compiler_params=params(63),
        cost_estimate=pl.CostEstimate(flops=128 << 20, bytes_accessed=2 << 20, transcendentals=0),
    )(start_offsets, taps, templates, channel_mask, jnp.asarray(order, jnp.bfloat16), raw_traces)
    rim = from_next_block(rim)
    exchanged = lax.all_to_all(message, ("y", "xl", "zp"), 0, 0, tiled=True)
    exchanged, rim = lax.optimization_barrier((exchanged, rim))
    gathered = lax.all_gather(exchanged, "zq", axis=0, tiled=True)
    gathered = gathered.reshape(blocks * ROWS, SUB * GROUP)

    traces = pl.pallas_call(
        trace_kernel,
        in_specs=[vmem()] * 5,
        out_specs=vmem(),
        out_shape=jax.ShapeDtypeStruct((GROUPS, GROUP, WIDE), jnp.float32),
        compiler_params=params(32),
        cost_estimate=pl.CostEstimate(flops=400 << 20, bytes_accessed=4 << 20, transcendentals=0),
    )(norm, raw_traces, rim, weights, jnp.repeat(station_shifts, 3)[:, None])
    traces = lax.all_to_all(traces, ("y", "xl"), 0, 0, tiled=True)

    powers = jnp.sum(traces[:, :, WIDE - 1], axis=0)
    norms = traces[:, USED, 0]
    facts = jnp.concatenate([powers, norms, jnp.zeros((LANES - GROUP - GROUPS,), jnp.float32)])
    along = lax.axis_size(("zq", "zp"))
    facts = jnp.broadcast_to(facts[None], (along, LANES))
    facts = lax.all_to_all(facts, ("zq", "zp"), 0, 0, tiled=True)
    powers = jnp.sum(facts[:, :GROUP], axis=0)
    root_power = jnp.sqrt(powers / (lags * blocks) + 1e-06)
    norms = facts[:, GROUP : GROUP + GROUPS].T.reshape(4, 1, 2 * along)
    norms = jnp.sum(lax.all_to_all(norms, ("xh", "core"), 0, 0, tiled=True), axis=(0, 1))
    root_power, norms = lax.optimization_barrier((root_power, norms))

    sums = correlate(gathered, traces, root_power[:, None], lags)
    sums = jnp.sum(lax.all_to_all(sums, "core", 0, 0, tiled=True), axis=0)
    sums = sums.astype(jnp.bfloat16).reshape(2 * GROUPS, 32, lags)
    sums = lax.all_to_all(sums, ("xh", "y", "xl"), 0, 0, tiled=True)
    sums = jnp.sum(sums.astype(jnp.float32), axis=0)
    return sums / jnp.sqrt(norms + 1e-05)[:, None]


def solution(mesh):
    fine = Mesh(
        mesh.devices.reshape(2, 4, 2, 8, 2, 2), ("xh", "y", "xl", "zq", "zp", "core")
    )
    parts = ("xh", "core")
    return jax.shard_map(
        local,
        mesh=fine,
        in_specs=(P(parts, BLK), P(), P(BLK, parts, None), P(BLK), P(BLK, parts), P(parts)),
        out_specs=P(parts, BLK),
        check_vma=False,
    )
```
